256 devices in a mesh: row: 8 (over z), col: 8 (over y, core), depth: 4 (over x).
Axes of the slice: x: 4, y: 4, z: 8, core: 2. Of those that a mesh axis runs over, the one named last changes fastest.
Arguments:
- p_blocks: bfloat16 [256, 64, 16384], P('row', None, 'col'), may hold values from -0.25 to 0.25
- p_cols: int32 [256, 256], P('row', 'col'), may hold values from -1 to 255, as said below
- out_mask: int32 [256, 8], P(('row', 'col', 'depth')), may hold values 0 or 1
Outputs:
- purified: float32 [256, 64, 512], P(('row', 'col', 'depth'))
The draws below stay inside these ranges and needn't reach their ends.
Inputs may be any that keep to these rules, and one draw needn't show every extreme that they name: `p_cols`: slot c * 32 + s of a block row holds a block column of c * 32 to (c + 1) * 32 - 1 or -1; the column numbers of a block row are distinct; within each group of 32 slots the used slots come first and at least one is used; in the group that holds a block row's own block column all 32 slots are used.
All inputs are finite; a program needn't handle non-finite values. No bound on the sum of `out_mask` on one device may be relied on, other than what follows from the above.
Results may differ from the reference program's by a relative error of at most 0.0027.
Values may be sent and summed in bfloat16 or wider, within the bound.
A program may use at most 128 MiB of HBM per device.

```python
import jax
import jax.numpy as jnp
from jax import lax

BS = 64
KS = 32
NB = 256
BC = 32
SLOTS = 256
WB = 8


def draw_p_cols(key, part):
    key = jax.random.fold_in(key, 11)
    key_order, key_count = jax.random.split(key)
    groups = NB // BC
    scores = jax.random.randint(key_order, (NB, groups, BC), 0, 1 << 20, dtype=jnp.int32)
    scores = scores * BC + jnp.arange(BC, dtype=jnp.int32)
    ordering = jnp.argsort(scores, axis=-1, stable=True).astype(jnp.int32)[:, :, :KS]
    home = jnp.arange(NB, dtype=jnp.int32) // BC
    group_ids = jnp.arange(groups, dtype=jnp.int32)
    apart = jnp.abs(group_ids[None, :] - home[:, None])
    apart = jnp.minimum(apart, groups - apart)
    cutting = jax.random.randint(key_count, (NB, groups), 0, KS + 1, dtype=jnp.int32)
    counts = jnp.maximum(1, KS - cutting * apart * 4 // groups)
    columns = ordering + group_ids[None, :, None] * BC
    slot_ids = jnp.arange(KS, dtype=jnp.int32)
    columns = jnp.where(slot_ids[None, None, :] < counts[:, :, None], columns, -1)
    return columns.reshape(NB, groups * KS).astype(jnp.int32)


def plant(drawn, key, low, high):
    shape = drawn.shape
    place = [jax.random.randint(jax.random.fold_in(key, axis), (), 0, shape[axis]) for axis in range(len(shape))]
    drawn = drawn.at[tuple(place)].set(low)
    longest = shape.index(max(shape))
    place[longest] = (place[longest] + 1) % shape[longest]
    return drawn.at[tuple(place)].set(high)


def shard_levels(own_key, dims, shards, least, largest):
    def one(dim, shards_of):
        steps = jax.random.uniform(jax.random.fold_in(jax.random.fold_in(own_key, 6), dim), (shards_of,), jnp.float32, least / len(shards), largest / len(shards))
        return jnp.repeat(jnp.exp(steps), dims[dim] // shards_of).reshape((-1,) + (1,) * (len(dims) - dim - 1))

    gain = one(*shards[0])
    for cut in shards[1:]:
        gain = gain * one(*cut)
    return gain


def bell_draw(rng, shape, deviation, reach, pieces=(), kind=jnp.bfloat16):
    array = deviation * jax.random.normal(rng, shape, jnp.float32)
    if pieces:
        array = array * shard_levels(rng, shape, pieces, -0.22, 0.18)
    return jnp.clip(array, -reach, reach).astype(kind)


def setup_inputs(seed: int = 0) -> dict:
    key_list = jax.random.split(jax.random.key(seed), 4)
    return {
        "p_blocks": bell_draw(key_list[0], (NB, BS, SLOTS * BS), (BS * SLOTS // 32) ** -0.5, 0.25, ((0, 8), (2, 8))),
        "p_cols": draw_p_cols(jax.random.fold_in(key_list[3], 71), 0),
        "out_mask": plant((jax.random.randint(key_list[2], (NB, WB), 0, 4) < 3).astype(jnp.int32), jax.random.fold_in(key_list[2], 1), 0, 1),
    }


def reference(p_blocks, p_cols, out_mask):
    block_count = p_cols.shape[0]
    slot_total = p_cols.shape[1]
    block_size = p_blocks.shape[1]
    window = out_mask.shape[1]
    panel_width = window // 2
    used_slot = p_cols >= 0
    clipped = jnp.where(used_slot, p_cols, 0).astype(jnp.int32)
    stored = p_blocks.astype(jnp.float32).reshape(block_count, block_size, slot_total, block_size)
    stored = stored.transpose(0, 2, 1, 3)
    stored = jnp.where(used_slot[:, :, None, None], stored, jnp.zeros((), jnp.float32))
    row_ids = jnp.broadcast_to(jnp.arange(block_count, dtype=jnp.int32)[:, None], clipped.shape)
    grid = jnp.zeros((block_count, block_count, block_size, block_size), jnp.float32)
    grid = grid.at[row_ids, clipped].add(stored)
    order = block_count * block_size
    matrix = grid.transpose(0, 2, 1, 3).reshape(order, order)
    first_cols = jnp.arange(panel_width * block_size, dtype=jnp.int32)
    columns = jnp.concatenate([first_cols, first_cols + (order // 2)]).astype(jnp.int32)
    panel = matrix[:, columns]
    square = jnp.dot(matrix, panel, precision=lax.Precision.HIGHEST)
    square_half = lax.optimization_barrier(square.astype(jnp.bfloat16))
    cube = jnp.dot(matrix, square_half.astype(jnp.float32), precision=lax.Precision.HIGHEST)
    result = 3.0 * square - 2.0 * cube
    result = result.reshape(block_count, block_size, window, block_size)
    result = result * out_mask.astype(jnp.float32)[:, None, :, None]
    return result.reshape(block_count, block_size, window * block_size)
```

```python
import functools

import jax
import jax.numpy as jnp
from jax import lax
from jax.experimental import pallas as pl
from jax.experimental.pallas import tpu as pltpu
from jax.sharding import PartitionSpec as P

MESH = pl.DeviceIdType.MESH
LANES = 128


def kernel(
    R, C, D, RB, BS, WB,
    p_hbm, codes, out,
    p, dense, panel, x1, x2, part, recv, square, rounded, cubes, owned,
    load_sem, scat_send, scat_recv, ag1_send, ag1_recv, rs_send, rs_recv,
    ag2_send, ag2_recv, sq_send, sq_recv, cu_send, cu_recv,
):
    r, c, d = lax.axis_index("row"), lax.axis_index("col"), lax.axis_index("depth")
    PB = RB // C
    PR = PB * BS
    K = RB * BS
    T = K // LANES
    half = D // 2
    cs = (d // half) * (C // 2)
    window = d % half

    def remote(src, dst, ss, rs, did):
        return pltpu.make_async_remote_copy(
            src_ref=src, dst_ref=dst, send_sem=ss, recv_sem=rs,
            device_id=did, device_id_type=MESH)

    def load(t):
        return pltpu.make_async_copy(
            p_hbm.at[:, :, pl.ds(t * LANES, LANES)], p.at[pl.ds(t * RB, RB)], load_sem.at[t])

    for t in range(T):
        load(t).start()

    barrier = pltpu.get_barrier_semaphore()

    def hello(did):
        pl.semaphore_signal(barrier, inc=1, device_id=did, device_id_type=MESH)

    for k in range(1, R):
        hello((lax.rem(r + k, R), c, d))
    for k in range(C):
        for e in range(D):
            if k or e:
                hello((r, lax.rem(c + k, C), lax.rem(d + e, D)))
    for k in range(R):
        @pl.when((lax.rem(r + k, R) != r) | (c != r))
        def _(k=k):
            hello((lax.rem(r + k, R), r, d))
    for k in range(C):
        @pl.when((lax.rem(c + k, C) != c) | (c != r))
        def _(k=k):
            hello((c, lax.rem(c + k, C), d))

    p[T * RB] = jnp.zeros((BS, LANES), jnp.bfloat16)
    n_hello = (R - 1) + (C * D - 1) + R + C
    pl.semaphore_wait(barrier, n_hello - 2 * jnp.where(r == c, 1, 0))

    left = lax.broadcasted_iota(jnp.int32, (BS, LANES), 1) < BS

    def placed(i, j):
        def pick(code):
            tile = p[code >> 1]
            moved = jnp.concatenate([tile[:, BS:], tile[:, :BS]], axis=1)
            return jnp.where(jnp.full((BS, LANES), code & 1) == 1, moved, tile)

        return jnp.where(left, pick(codes[i, 2 * j]), pick(codes[i, 2 * j + 1]))

    for t in range(T):
        load(t).wait()

    @pl.when(c == cs)
    def _():
        for q in range(C):
            def extract(j, _, q=q):
                panel[q, pl.ds(pl.multiple_of(j * BS, BS), BS), :] = placed(q * PB + j, window)
                return 0

            lax.fori_loop(0, PB, extract, 0)
            dst = x1.at[pl.ds(q * PR, PR)]

            @pl.when((q == r) & (r == c))
            def _(q=q, dst=dst):
                pltpu.make_async_copy(panel.at[q], dst, scat_recv).start()

            @pl.when((q != r) | (r != c))
            def _(q=q, dst=dst):
                remote(panel.at[q], dst, scat_send.at[q], scat_recv, (q, r, d)).start()

    def densify(i, _):
        rows = pl.ds(pl.multiple_of(i * BS, BS), BS)
        for j in range(T):
            dense[rows, j * LANES:(j + 1) * LANES] = placed(i, j)
        return 0

    lax.fori_loop(0, RB, densify, 0)

    mine = x1.at[pl.ds(pl.multiple_of(r * PR, PR), PR)]
    pltpu.make_async_copy(mine, mine, scat_recv).wait()

    def gather1(k):
        return remote(mine, mine, ag1_send.at[k], ag1_recv.at[k], (lax.rem(r + k, R), c, d))

    order = sorted(range(1, R), key=lambda k: -min(k, R - k))
    for k in order:
        gather1(k).start()
    def term(x, q, piece):
        at = pl.multiple_of(piece * PR, PR)
        return jnp.dot(
            dense[pl.ds(pl.multiple_of(q * PR, PR), PR), pl.ds(at, PR)], x[pl.ds(at, PR), :],
            preferred_element_type=jnp.float32)

    def first(x, piece):
        def one(q, _):
            part[q] = term(x, q, piece)
            return 0

        lax.fori_loop(0, C, one, 0)

    def more(x, piece):
        def one(q, _):
            part[q] += term(x, q, piece)
            return 0

        lax.fori_loop(0, C, one, 0)

    first(x1, r)
    near = order[::-1]
    for k in near:
        gather1(k).wait_recv()
        if k != near[-1]:
            more(x1, lax.rem(r + R - k, R))

    def reduce1(k):
        q = lax.rem(c + k, C)
        return remote(part.at[q], recv.at[c], rs_send.at[k], rs_recv.at[k], (r, q, d))

    for k in [*range(1, C), 0]:
        q = lax.rem(c + k, C)
        part[q] += term(x1, q, lax.rem(r + R - near[-1], R))
        if k:
            reduce1(k).start()
    total = part[c]
    for k in range(1, C):
        src = lax.rem(c + C - k, C)
        remote(part.at[0], recv.at[src], rs_send.at[k], rs_recv.at[k], (r, c, d)).wait_recv()
        total = total + recv[src]
    square[...] = total
    slot = pl.ds(pl.multiple_of(c * PR, PR), PR)
    rounded[...] = total.astype(jnp.bfloat16)

    def gather2(k):
        z = lax.rem(r + k, R)
        return remote(rounded, x2.at[slot], ag2_send.at[k], ag2_recv.at[c], (z, r, d))

    for k in order:
        gather2(k).start()

    @pl.when(r == c)
    def _():
        pltpu.make_async_copy(rounded, x2.at[slot], ag2_recv.at[c]).start()

    @pl.when(r != c)
    def _():
        gather2(0).start()

    def give(e):
        return remote(
            square.at[pl.ds(pl.multiple_of(lax.rem(d + e, D) * BS, BS), BS)], owned.at[d],
            sq_send.at[e], sq_recv.at[e], (r, c, lax.rem(d + e, D)))

    for e in range(1, D):
        give(e).start()
    for k in range(1, C):
        reduce1(k).wait_send()
    for q in range(C):
        piece = x2.at[pl.ds(q * PR, PR)]
        pltpu.make_async_copy(piece, piece, ag2_recv.at[q]).wait()
        if q == 0:
            first(x2, q)
        elif q < C - 1:
            more(x2, q)

    def blockrow(q, e):
        return part.at[q, pl.ds(pl.multiple_of(e * BS, BS), BS)]

    def cube(k, e):
        q, to = lax.rem(c + k, C), lax.rem(d + e, D)
        return remote(
            blockrow(q, to), cubes.at[c * D + d], cu_send.at[k * D + e], cu_recv, (r, q, to))

    for k in [*range(1, C), 0]:
        q = lax.rem(c + k, C)
        part[q] += term(x2, q, C - 1)
        for e in [2, 1, 3, 0]:
            if k or e:
                cube(k, e).start()
    pltpu.make_async_copy(blockrow(c, d), cubes.at[c * D + d], cu_recv).start()
    pltpu.make_async_copy(cubes, cubes, cu_recv).wait()
    own = square[pl.ds(pl.multiple_of(d * BS, BS), BS), :]
    for e in range(1, D):
        give(e).wait_recv()
    for e in range(D):
        sq = jnp.where(d == e, own, owned[e])
        total = cubes[e]
        for q in range(1, C):
            total = total + cubes[q * D + e]
        out[:, e * LANES:(e + 1) * LANES] = 3.0 * sq - 2.0 * total

    @pl.when(c == cs)
    def _():
        for q in range(C):
            @pl.when((q != r) | (r != c))
            def _(q=q):
                remote(panel.at[q], panel.at[q], scat_send.at[q], scat_recv, (q, r, d)).wait_send()

    for k in order:
        gather1(k).wait_send()
        gather2(k).wait_send()

    @pl.when(r != c)
    def _():
        gather2(0).wait_send()

    for e in range(1, D):
        give(e).wait_send()
    for k in range(C):
        for e in range(D):
            if k or e:
                cube(k, e).wait_send()


def body(p_blocks, p_cols, out_mask):
    R, C, D = lax.axis_size("row"), lax.axis_size("col"), lax.axis_size("depth")
    RB, BS, K = p_blocks.shape
    WB = out_mask.shape[1]
    PR = RB // C * BS
    bf, f32 = jnp.bfloat16, jnp.float32
    dma = pltpu.SemaphoreType.DMA
    T = K // LANES
    places = jnp.arange(RB, dtype=jnp.int32)
    wanted = lax.axis_index("col") * RB + places
    slot = jnp.max(
        jnp.where(p_cols[:, :, None] == wanted, places[None, :, None], -1), axis=1)
    tile = (slot // 2) * RB + places[:, None]
    codes = jnp.where(slot < 0, 2 * T * RB, 2 * tile + (slot % 2 != places % 2))
    rows = pl.pallas_call(
        functools.partial(kernel, R, C, D, RB, BS, WB),
        out_shape=jax.ShapeDtypeStruct((BS, WB * BS), f32),
        in_specs=[pl.BlockSpec(memory_space=pl.ANY), pl.BlockSpec(memory_space=pltpu.SMEM)],
        out_specs=pl.BlockSpec(memory_space=pltpu.VMEM),
        scratch_shapes=[
            pltpu.VMEM((T * RB + 1, BS, LANES), bf),
            pltpu.VMEM((K, K), bf),
            pltpu.VMEM((C, PR, LANES), bf),
            pltpu.VMEM((K, LANES), bf),
            pltpu.VMEM((K, LANES), bf),
            pltpu.VMEM((C, PR, LANES), f32),
            pltpu.VMEM((C, PR, LANES), f32),
            pltpu.VMEM((PR, LANES), f32),
            pltpu.VMEM((PR, LANES), bf),
            pltpu.VMEM((C * D, BS, LANES), f32),
            pltpu.VMEM((D, BS, LANES), f32),
            dma((T,)), dma((C,)), dma, dma((R,)), dma((R,)), dma((C,)), dma((C,)),
            dma((R,)), dma((C,)), dma((D,)), dma((D,)), dma((C * D,)), dma,
        ],
        compiler_params=pltpu.CompilerParams(
            collective_id=0, has_side_effects=True, vmem_limit_bytes=48 << 20),
    )(p_blocks, codes)
    shaped = rows.reshape(1, BS, WB, BS) * out_mask.astype(f32)[:, None, :, None]
    return shaped.reshape(1, BS, WB * BS)


def solution(mesh):
    in_specs = (P("row", None, "col"), P("row", "col"), P(("row", "col", "depth"), None))
    out_specs = P(("row", "col", "depth"), None, None)
    return jax.shard_map(body, mesh=mesh, in_specs=in_specs, out_specs=out_specs, check_vma=False)
```

```python
import functools

import jax
import jax.numpy as jnp
from jax import lax
from jax.experimental import pallas as pl
from jax.experimental.pallas import tpu as pltpu
from jax.sharding import PartitionSpec as P

MESH = pl.DeviceIdType.MESH
LANES = 128


def kernel(
    R, C, D, RB, BS,
    p_hbm, codes, out,
    p, dense, panel, x1, x2, part, core1, core2, recv, square, rounded, cubes, owned,
    load_sem, scat_send, in1, ag1_send, ag1_recv, core1_send, core1_recv, rs_send, rs_recv,
    turn_send, in2, ag2_send, ag2_recv, sq_send, sq_recv, core2_send, core2_recv,
    cu_send, cu_recv,
):
    r, c, d = lax.axis_index("row"), lax.axis_index("col"), lax.axis_index("depth")
    PB = RB // C
    PR = PB * BS
    K = RB * BS
    T = K // LANES
    H, Y, half, each = R // 2, C // 2, D // 2, C // D
    y, core = c // 2, lax.rem(c, 2)
    sibling = (r, c + 1 - 2 * core, d)
    side = c // Y
    source = lax.rem(c, Y) == 0

    def remote(src, dst, ss, rs, did):
        return pltpu.make_async_remote_copy(
            src_ref=src, dst_ref=dst, send_sem=ss, recv_sem=rs,
            device_id=did, device_id_type=MESH)

    def is_self(did):
        return (did[0] == r) & (did[1] == c) & (did[2] == d)

    def piece_of(x, q):
        return x.at[pl.ds(pl.multiple_of(q * PR, PR), PR)]

    def load(t):
        return pltpu.make_async_copy(
            p_hbm.at[:, :, pl.ds(t * LANES, LANES)], p.at[pl.ds(t * RB, RB)], load_sem.at[t])

    for t in range(T):
        load(t).start()

    scatter = []
    for u in range(each):
        for w in range(half):
            for v in range(2):
                q = d * each + u
                scatter.append((u, w, v, q, (lax.rem(q + v * H, R), r, side * half + w)))
    hops = [k for n in range(H // 2, 0, -1) for k in (n, R - n)]
    hops = list(dict.fromkeys(hops))
    turned = [(lax.rem(c + v * H, R), r, d) for v in range(2)]

    barrier = pltpu.get_barrier_semaphore()

    def hello(did):
        pl.semaphore_signal(barrier, inc=1, device_id=did, device_id_type=MESH)

    def hello_other(did):
        @pl.when(jnp.logical_not(is_self(did)))
        def _():
            hello(did)

    for v in range(2):
        q = lax.rem(r + v * H, R)
        hello_other((c, (d // half) * Y, q // each))
        hello_other((c, q, d))
    for k in hops:
        hello((lax.rem(r + k, R), c, d))
    hello(sibling)
    for k in range(Y):
        for e in range(D):
            if k or e:
                hello((r, 2 * lax.rem(y + k, Y) + core, lax.rem(d + e, D)))

    def others(dids):
        return sum(jnp.where(is_self(did), 0, 1) for did in dids)

    p[T * RB] = jnp.zeros((BS, LANES), jnp.bfloat16)
    panels = others([s[-1] for s in scatter])
    pl.semaphore_wait(
        barrier, len(hops) + Y * D + others(turned) + jnp.where(source, panels, 0))

    left = lax.broadcasted_iota(jnp.int32, (BS, LANES), 1) < BS

    def placed(i, j):
        def pick(code):
            tile = p[code >> 1]
            moved = jnp.concatenate([tile[:, BS:], tile[:, :BS]], axis=1)
            return jnp.where(jnp.full((BS, LANES), code & 1) == 1, moved, tile)

        return jnp.where(left, pick(codes[i, 2 * j]), pick(codes[i, 2 * j + 1]))

    for t in range(T):
        load(t).wait()

    def panel_copy(u, w, v, q, did):
        return remote(panel.at[u, w], piece_of(x1, q), scat_send.at[u, w, v], in1.at[v], did)

    @pl.when(source)
    def _():
        for u in range(each):
            def extract(j, _, u=u):
                rows = pl.ds(pl.multiple_of(j * BS, BS), BS)
                for w in range(half):
                    panel[u, w, rows, :] = placed((d * each + u) * PB + j, w)
                return 0

            lax.fori_loop(0, PB, extract, 0)
            for s in scatter:
                if s[0] == u:
                    @pl.when(is_self(s[-1]))
                    def _(s=s):
                        pltpu.make_async_copy(
                            panel.at[s[0], s[1]], piece_of(x1, s[3]), in1.at[s[2]]).start()

                    @pl.when(jnp.logical_not(is_self(s[-1])))
                    def _(s=s):
                        panel_copy(*s).start()

    def densify(i, _):
        rows = pl.ds(pl.multiple_of(i * BS, BS), BS)
        for j in range(T):
            dense[rows, j * LANES:(j + 1) * LANES] = placed(i, j)
        return 0

    lax.fori_loop(0, RB, densify, 0)

    def spread(x, arrived, sends, recvs):
        def copy(v, k):
            at = piece_of(x, lax.rem(r + v * H, R))
            return remote(at, at, sends.at[v, k], recvs.at[v, k], (lax.rem(r + k, R), c, d))

        moves = [(v, k) for v in range(2) for k in hops if v == 0 or 2 * min(k, R - k) < H]
        for v in range(2):
            at = piece_of(x, lax.rem(r + v * H, R))
            pltpu.make_async_copy(at, at, arrived.at[v]).wait()
            for move in moves:
                if move[0] == v:
                    copy(*move).start()
        for move in moves:
            copy(*move).wait_recv()
        return [copy(*move) for move in moves]

    def product(x, q):
        rows = pl.ds(pl.multiple_of(q * PR, PR), PR)
        part[q] = jnp.dot(dense[rows, :], x[...], preferred_element_type=jnp.float32)

    far = sorted(range(1, Y), key=lambda k: -min(k, Y - k)) + [0]

    def to_sibling(x, k, buffer, sends, recvs):
        m = lax.rem(y + k, Y)
        q = 2 * m + 1 - core
        return q, remote(part.at[q], buffer.at[k], sends.at[k], recvs.at[k], sibling)

    def with_sibling(x, buffer, sends, recvs, then):
        for k in far:
            q, copy = to_sibling(x, k, buffer, sends, recvs)
            product(x, q)
            copy.start()
        for k in far:
            q = 2 * lax.rem(y + k, Y) + core
            product(x, q)
            to_sibling(x, k, buffer, sends, recvs)[1].wait_recv()
            part[q] += buffer[k]
            then(k, q)

    sent1 = spread(x1, in1, ag1_send, ag1_recv)

    def reduce1(k):
        q = 2 * lax.rem(y + k, Y) + core
        return remote(part.at[q], recv.at[k], rs_send.at[k], rs_recv.at[k], (r, q, d))

    def send1(k, q):
        if k:
            reduce1(k).start()

    with_sibling(x1, core1, core1_send, core1_recv, send1)
    total = part[c]
    for k in range(1, Y):
        reduce1(k).wait_recv()
        total = total + recv[k]
    square[...] = total
    rounded[...] = total.astype(jnp.bfloat16)

    def turn(v):
        return remote(rounded, piece_of(x2, c), turn_send.at[v], in2.at[v], turned[v])

    for v in range(2):
        @pl.when(is_self(turned[v]))
        def _(v=v):
            pltpu.make_async_copy(rounded, piece_of(x2, c), in2.at[v]).start()

        @pl.when(jnp.logical_not(is_self(turned[v])))
        def _(v=v):
            turn(v).start()

    def give(e):
        to = lax.rem(d + e, D)
        return remote(
            square.at[pl.ds(pl.multiple_of(to * BS, BS), BS)], owned.at[d],
            sq_send.at[e], sq_recv.at[e], (r, c, to))

    sent2 = spread(x2, in2, ag2_send, ag2_recv)
    for e in range(1, D):
        give(e).start()
    for k in range(Y):
        to_sibling(x1, k, core1, core1_send, core1_recv)[1].wait_send()
        if k:
            reduce1(k).wait_send()

    def cube(k, e):
        q, to = 2 * lax.rem(y + k, Y) + core, lax.rem(d + e, D)
        return remote(
            part.at[q, pl.ds(pl.multiple_of(to * BS, BS), BS)], cubes.at[y * D + d],
            cu_send.at[k * D + e], cu_recv, (r, q, to))

    def send2(k, q):
        for e in sorted(range(D), key=lambda e: -min(e, D - e)):
            if k or e:
                cube(k, e).start()
            else:
                pltpu.make_async_copy(
                    part.at[q, pl.ds(pl.multiple_of(d * BS, BS), BS)], cubes.at[y * D + d],
                    cu_recv).start()

    with_sibling(x2, core2, core2_send, core2_recv, send2)
    for e in range(1, D):
        give(e).wait_recv()
    pltpu.make_async_copy(cubes, cubes, cu_recv).wait()
    own = square[pl.ds(pl.multiple_of(d * BS, BS), BS), :]
    for e in range(D):
        total = cubes[e]
        for m in range(1, Y):
            total = total + cubes[m * D + e]
        out[:, e * LANES:(e + 1) * LANES] = 3.0 * jnp.where(d == e, own, owned[e]) - 2.0 * total

    @pl.when(source)
    def _():
        for s in scatter:
            @pl.when(jnp.logical_not(is_self(s[-1])))
            def _(s=s):
                panel_copy(*s).wait_send()

    for copy in sent1 + sent2:
        copy.wait_send()
    for v in range(2):
        @pl.when(jnp.logical_not(is_self(turned[v])))
        def _(v=v):
            turn(v).wait_send()

    for e in range(1, D):
        give(e).wait_send()
    for k in range(Y):
        to_sibling(x2, k, core2, core2_send, core2_recv)[1].wait_send()
        for e in range(D):
            if k or e:
                cube(k, e).wait_send()


def body(p_blocks, p_cols, out_mask):
    R, C, D = lax.axis_size("row"), lax.axis_size("col"), lax.axis_size("depth")
    RB, BS, K = p_blocks.shape
    WB = out_mask.shape[1]
    PR = RB // C * BS
    T, Y = K // LANES, C // 2
    bf, f32 = jnp.bfloat16, jnp.float32
    dma = pltpu.SemaphoreType.DMA
    places = jnp.arange(RB, dtype=jnp.int32)
    wanted = lax.axis_index("col") * RB + places
    slot = jnp.max(
        jnp.where(p_cols[:, :, None] == wanted, places[None, :, None], -1), axis=1)
    tile = (slot // 2) * RB + places[:, None]
    codes = jnp.where(slot < 0, 2 * T * RB, 2 * tile + (slot % 2 != places % 2))
    rows = pl.pallas_call(
        functools.partial(kernel, R, C, D, RB, BS),
        out_shape=jax.ShapeDtypeStruct((BS, WB * BS), f32),
        in_specs=[pl.BlockSpec(memory_space=pl.ANY), pl.BlockSpec(memory_space=pltpu.SMEM)],
        out_specs=pl.BlockSpec(memory_space=pltpu.VMEM),
        scratch_shapes=[
            pltpu.VMEM((T * RB + 1, BS, LANES), bf),
            pltpu.VMEM((K, K), bf),
            pltpu.VMEM((C // D, D // 2, PR, LANES), bf),
            pltpu.VMEM((K, LANES), bf),
            pltpu.VMEM((K, LANES), bf),
            pltpu.VMEM((C, PR, LANES), f32),
            pltpu.VMEM((Y, PR, LANES), f32),
            pltpu.VMEM((Y, PR, LANES), f32),
            pltpu.VMEM((Y, PR, LANES), f32),
            pltpu.VMEM((PR, LANES), f32),
            pltpu.VMEM((PR, LANES), bf),
            pltpu.VMEM((Y * D, BS, LANES), f32),
            pltpu.VMEM((D, BS, LANES), f32),
            dma((T,)), dma((C // D, D // 2, 2)), dma((2,)), dma((2, R)), dma((2, R)),
            dma((Y,)), dma((Y,)), dma((Y,)), dma((Y,)),
            dma((2,)), dma((2,)), dma((2, R)), dma((2, R)), dma((D,)), dma((D,)),
            dma((Y,)), dma((Y,)), dma((Y * D,)), dma,
        ],
        compiler_params=pltpu.CompilerParams(
            collective_id=0, has_side_effects=True, vmem_limit_bytes=48 << 20),
    )(p_blocks, codes)
    shaped = rows.reshape(1, BS, WB, BS) * out_mask.astype(f32)[:, None, :, None]
    return shaped.reshape(1, BS, WB * BS)


def solution(mesh):
    in_specs = (P("row", None, "col"), P("row", "col"), P(("row", "col", "depth"), None))
    out_specs = P(("row", "col", "depth"), None, None)
    return jax.shard_map(body, mesh=mesh, in_specs=in_specs, out_specs=out_specs, check_vma=False)
```

```python
import functools

import jax
import jax.numpy as jnp
from jax import lax
from jax.experimental import pallas as pl
from jax.experimental.pallas import tpu as pltpu
from jax.sharding import PartitionSpec as P

MESH = pl.DeviceIdType.MESH
LANES = 128


def kernel(
    R, C, D, RB, BS,
    p_hbm, cols, out,
    table, codes, p, dense, panel, x1, x2, part, core1, core2, sent, recv, square, rounded, shares, cubes, owned,
    table_sem, load_sem, scat_send, in1, ag1_send, ag1_recv, core1_send, core1_recv, rs_send, rs_recv,
    turn_send, in2, ag2_send, ag2_recv, sq_send, sq_recv, core2_send, core2_recv,
    cu_send, cu_recv,
):
    r, c, d = lax.axis_index("row"), lax.axis_index("col"), lax.axis_index("depth")
    PB = RB // C
    PR = PB * BS
    K = RB * BS
    T = K // LANES
    H, Y, half = R // 2, C // 2, D // 2
    y, core = c // 2, lax.rem(c, 2)
    sibling = (r, c + 1 - 2 * core, d)
    side = c // Y
    source = lax.rem(c, Y) == 0

    def remote(src, dst, ss, rs, did):
        return pltpu.make_async_remote_copy(
            src_ref=src, dst_ref=dst, send_sem=ss, recv_sem=rs,
            device_id=did, device_id_type=MESH)

    def is_self(did):
        return (did[0] == r) & (did[1] == c) & (did[2] == d)

    def piece_of(x, q):
        return x.at[pl.ds(pl.multiple_of(q * PR, PR), PR)]

    def block_of(x, i):
        return x.at[pl.ds(pl.multiple_of(i * BS, BS), BS)]

    def load(t):
        return pltpu.make_async_copy(
            p_hbm.at[:, :, pl.ds(t * LANES, LANES)], p.at[pl.ds(t * RB, RB)], load_sem.at[t])

    scatter = [
        (q, w, v, ((q + v * H) % R, r, side * half + w))
        for q in range(C) for v in range(2) for w in range(half)]
    receivers = [(z, r, side * half + w) for z in range(R) for w in range(half)]
    hops = [k for n in range(H // 2, 0, -1) for k in (n, R - n)]
    hops = list(dict.fromkeys(hops))
    turned = [(lax.rem(c + v * H, R), r, d) for v in range(2)]

    barrier = pltpu.get_barrier_semaphore()

    def hello(did):
        pl.semaphore_signal(barrier, inc=1, device_id=did, device_id_type=MESH)

    def hello_other(did):
        @pl.when(jnp.logical_not(is_self(did)))
        def _():
            hello(did)

    for e in range(D):
        hello_other((c, (d // half) * Y, lax.rem(d + e, D)))
    for v in range(2):
        hello_other((c, lax.rem(r + v * H, R), d))
    for k in hops:
        hello((lax.rem(r + k, R), c, d))
    hello(sibling)
    for k in range(Y):
        for e in range(D):
            if k or e:
                hello((r, 2 * lax.rem(y + k, Y) + core, lax.rem(d + e, D)))

    def others(dids):
        return sum(jnp.where(is_self(did), 0, 1) for did in dids)

    for t in range(T):
        load(t).start()

    row = lax.broadcasted_iota(jnp.int32, (RB, LANES), 0)
    place = lax.broadcasted_iota(jnp.int32, (RB, LANES), 1)
    local = cols[...] - c * RB
    code = jnp.full((RB, LANES), 2 * T * RB, jnp.int32)
    for u in range(RB):
        at = 2 * ((u // 2) * RB + row) + ((place & 1) ^ (u & 1))
        code = jnp.where(local[:, u:u + 1] == place, at, code)
    table[...] = code
    fill = pltpu.make_async_copy(table, codes, table_sem)
    fill.start()
    p[T * RB] = jnp.zeros((BS, LANES), jnp.bfloat16)
    fill.wait()
    panels = others(receivers)
    pl.semaphore_wait(
        barrier, len(hops) + Y * D + others(turned) + jnp.where(source, panels, 0))

    left = lax.broadcasted_iota(jnp.int32, (BS, LANES), 1) < BS

    def placed(i, j):
        def pick(code):
            tile = p[code >> 1]
            moved = jnp.concatenate([tile[:, BS:], tile[:, :BS]], axis=1)
            return jnp.where(jnp.full((BS, LANES), code & 1) == 1, moved, tile)

        return jnp.where(left, pick(codes[i, 2 * j]), pick(codes[i, 2 * j + 1]))

    for t in range(T):
        load(t).wait()

    def panel_copy(q, w, v, did):
        return remote(
            panel.at[q, w], block_of(x1, q * PB + d), scat_send.at[q, w, v], in1.at[v], did)

    @pl.when(source)
    def _():
        def extract(q, _):
            for w in range(half):
                panel[q, w] = placed(q * PB + d, w)
            return 0

        lax.fori_loop(0, C, extract, 0)
        for s in scatter:
            @pl.when(is_self(s[-1]))
            def _(s=s):
                pltpu.make_async_copy(
                    panel.at[s[0], s[1]], block_of(x1, s[0] * PB + d), in1.at[s[2]]).start()

            @pl.when(jnp.logical_not(is_self(s[-1])))
            def _(s=s):
                panel_copy(*s).start()

    def densify(i, _):
        rows = pl.ds(pl.multiple_of(i * BS, BS), BS)
        for j in range(T):
            dense[rows, j * LANES:(j + 1) * LANES] = placed(i, j)
        return 0

    lax.fori_loop(0, RB, densify, 0)

    def spread(x, arrived, sends, recvs):
        def copy(v, k):
            at = piece_of(x, lax.rem(r + v * H, R))
            return remote(at, at, sends.at[v, k], recvs.at[v, k], (lax.rem(r + k, R), c, d))

        moves = [(v, k) for v in range(2) for k in hops if v == 0 or 2 * min(k, R - k) < H]
        for v in range(2):
            at = piece_of(x, lax.rem(r + v * H, R))
            pltpu.make_async_copy(at, at, arrived.at[v]).wait()
            for move in moves:
                if move[0] == v:
                    copy(*move).start()
        for move in moves:
            copy(*move).wait_recv()
        return [copy(*move) for move in moves]

    def product(x, q):
        rows = pl.ds(pl.multiple_of(q * PR, PR), PR)
        part[q] = jnp.dot(dense[rows, :], x[...], preferred_element_type=jnp.float32)

    def coded(value, ref):
        n = value.shape[0]
        top = jnp.maximum(jnp.max(jnp.abs(value), axis=0, keepdims=True), 1e-30)
        level = jnp.ceil(jnp.log2(top) * 16.0) + 1.0
        scaled = jnp.round(value * (jnp.exp2(level * -0.0625) * 32000.0))
        ref[0:n, :] = scaled.astype(jnp.int32).astype(jnp.int16)
        ref[n:n + 16, :] = jnp.broadcast_to(
            level, (16, LANES)).astype(jnp.int32).astype(jnp.int16)

    def decoded(ref, n):
        level = ref[n:n + 16, :].astype(jnp.int32).astype(jnp.float32)[0:1, :]
        scale = jnp.exp2(level * 0.0625) * (1.0 / 32000.0)
        return ref[0:n, :].astype(jnp.int32).astype(jnp.float32) * scale

    far = sorted(range(1, Y), key=lambda k: -min(k, Y - k)) + [0]

    def to_sibling(x, k, buffer, sends, recvs):
        m = lax.rem(y + k, Y)
        q = 2 * m + 1 - core
        return q, remote(part.at[q], buffer.at[k], sends.at[k], recvs.at[k], sibling)

    def with_sibling(x, buffer, sends, recvs, then):
        for k in far:
            q, copy = to_sibling(x, k, buffer, sends, recvs)
            product(x, q)
            copy.start()
        for k in far:
            q = 2 * lax.rem(y + k, Y) + core
            product(x, q)
            to_sibling(x, k, buffer, sends, recvs)[1].wait_recv()
            then(k, q, part[q] + buffer[k])

    sent1 = spread(x1, in1, ag1_send, ag1_recv)

    def reduce1(k):
        q = 2 * lax.rem(y + k, Y) + core
        return remote(sent.at[k], recv.at[k], rs_send.at[k], rs_recv.at[k], (r, q, d))

    def send1(k, q, value):
        if k:
            coded(value, sent.at[k])
            reduce1(k).start()
        else:
            square[...] = value

    with_sibling(x1, core1, core1_send, core1_recv, send1)
    total = square[...]
    for k in range(1, Y):
        reduce1(k).wait_recv()
        total = total + decoded(recv.at[k], PR)
    square[...] = total
    rounded[...] = total.astype(jnp.bfloat16)

    def turn(v):
        return remote(rounded, piece_of(x2, c), turn_send.at[v], in2.at[v], turned[v])

    for v in range(2):
        @pl.when(is_self(turned[v]))
        def _(v=v):
            pltpu.make_async_copy(rounded, piece_of(x2, c), in2.at[v]).start()

        @pl.when(jnp.logical_not(is_self(turned[v])))
        def _(v=v):
            turn(v).start()

    def give(e):
        to = lax.rem(d + e, D)
        return remote(
            square.at[pl.ds(pl.multiple_of(to * BS, BS), BS)], owned.at[d],
            sq_send.at[e], sq_recv.at[e], (r, c, to))

    sent2 = spread(x2, in2, ag2_send, ag2_recv)
    for e in range(1, D):
        give(e).start()
    for k in range(Y):
        to_sibling(x1, k, core1, core1_send, core1_recv)[1].wait_send()
        if k:
            reduce1(k).wait_send()

    def cube(k, e):
        q, to = 2 * lax.rem(y + k, Y) + core, lax.rem(d + e, D)
        return remote(
            shares.at[k * D + e], cubes.at[y * D + d],
            cu_send.at[k * D + e], cu_recv, (r, q, to))

    def send2(k, q, value):
        part[q] = value
        for e in sorted(range(D), key=lambda e: -min(e, D - e)):
            to = pl.ds(pl.multiple_of(lax.rem(d + e, D) * BS, BS), BS)
            coded(part[q, to, :], shares.at[k * D + e])
            if k or e:
                cube(k, e).start()
            else:
                pltpu.make_async_copy(shares.at[0], cubes.at[y * D + d], cu_recv).start()

    with_sibling(x2, core2, core2_send, core2_recv, send2)
    for e in range(1, D):
        give(e).wait_recv()
    pltpu.make_async_copy(cubes, cubes, cu_recv).wait()
    own = square[pl.ds(pl.multiple_of(d * BS, BS), BS), :]
    for e in range(D):
        total = decoded(cubes.at[e], BS)
        for m in range(1, Y):
            total = total + decoded(cubes.at[m * D + e], BS)
        out[:, e * LANES:(e + 1) * LANES] = 3.0 * jnp.where(d == e, own, owned[e]) - 2.0 * total

    @pl.when(source)
    def _():
        for s in scatter:
            @pl.when(jnp.logical_not(is_self(s[-1])))
            def _(s=s):
                panel_copy(*s).wait_send()

    for copy in sent1 + sent2:
        copy.wait_send()
    for v in range(2):
        @pl.when(jnp.logical_not(is_self(turned[v])))
        def _(v=v):
            turn(v).wait_send()

    for e in range(1, D):
        give(e).wait_send()
    for k in range(Y):
        to_sibling(x2, k, core2, core2_send, core2_recv)[1].wait_send()
        for e in range(D):
            if k or e:
                cube(k, e).wait_send()


def body(p_blocks, p_cols, out_mask):
    R, C, D = lax.axis_size("row"), lax.axis_size("col"), lax.axis_size("depth")
    RB, BS, K = p_blocks.shape
    WB = out_mask.shape[1]
    PR = RB // C * BS
    T, Y = K // LANES, C // 2
    bf, f32 = jnp.bfloat16, jnp.float32
    dma = pltpu.SemaphoreType.DMA
    rows = pl.pallas_call(
        functools.partial(kernel, R, C, D, RB, BS),
        out_shape=jax.ShapeDtypeStruct((BS, WB * BS), f32),
        in_specs=[pl.BlockSpec(memory_space=pl.ANY), pl.BlockSpec(memory_space=pltpu.VMEM)],
        out_specs=pl.BlockSpec(memory_space=pltpu.VMEM),
        scratch_shapes=[
            pltpu.VMEM((RB, LANES), jnp.int32),
            pltpu.SMEM((RB, LANES), jnp.int32),
            pltpu.VMEM((T * RB + 1, BS, LANES), bf),
            pltpu.VMEM((K, K), bf),
            pltpu.VMEM((C, D // 2, BS, LANES), bf),
            pltpu.VMEM((K, LANES), bf),
            pltpu.VMEM((K, LANES), bf),
            pltpu.VMEM((C, PR, LANES), f32),
            pltpu.VMEM((Y, PR, LANES), f32),
            pltpu.VMEM((Y, PR, LANES), f32),
            pltpu.VMEM((Y, PR + 16, LANES), jnp.int16),
            pltpu.VMEM((Y, PR + 16, LANES), jnp.int16),
            pltpu.VMEM((PR, LANES), f32),
            pltpu.VMEM((PR, LANES), bf),
            pltpu.VMEM((Y * D, BS + 16, LANES), jnp.int16),
            pltpu.VMEM((Y * D, BS + 16, LANES), jnp.int16),
            pltpu.VMEM((D, BS, LANES), f32),
            dma, dma((T,)), dma((C, D // 2, 2)), dma((2,)), dma((2, R)), dma((2, R)),
            dma((Y,)), dma((Y,)), dma((Y,)), dma((Y,)),
            dma((2,)), dma((2,)), dma((2, R)), dma((2, R)), dma((D,)), dma((D,)),
            dma((Y,)), dma((Y,)), dma((Y * D,)), dma,
        ],
        compiler_params=pltpu.CompilerParams(
            collective_id=0, has_side_effects=True, vmem_limit_bytes=48 << 20),
    )(p_blocks, p_cols)
    shaped = rows.reshape(1, BS, WB, BS) * out_mask.astype(f32)[:, None, :, None]
    return shaped.reshape(1, BS, WB * BS)


def solution(mesh):
    in_specs = (P("row", None, "col"), P("row", "col"), P(("row", "col", "depth"), None))
    out_specs = P(("row", "col", "depth"), None, None)
    return jax.shard_map(body, mesh=mesh, in_specs=in_specs, out_specs=out_specs, check_vma=False)
```

```python
import functools

import jax
import jax.numpy as jnp
from jax import lax
from jax.experimental import pallas as pl
from jax.experimental.pallas import tpu as pltpu
from jax.sharding import PartitionSpec as P

MESH = pl.DeviceIdType.MESH
LANES = 128


def kernel(
    R, C, D, RB, BS,
    p_hbm, cols, out,
    table, codes, p, dense, panel, x1, x2, part, core1, core2, sent, recv, square, rounded, shares, cubes, owned,
    table_sem, load_sem, scat_send, in1, ag1_send, ag1_recv, core1_send, core1_recv, rs_send, rs_recv,
    turn_send, in2, ag2_send, ag2_recv, sq_send, sq_recv, core2_send, core2_recv,
    cu_send, cu_recv,
):
    r, c, d = lax.axis_index("row"), lax.axis_index("col"), lax.axis_index("depth")
    PB = RB // C
    PR = PB * BS
    K = RB * BS
    T = K // LANES
    H, Y, half = R // 2, C // 2, D // 2
    y, core = c // 2, lax.rem(c, 2)
    sibling = (r, c + 1 - 2 * core, d)
    side = c // Y
    source = lax.rem(c, Y) == 0

    def remote(src, dst, ss, rs, did):
        return pltpu.make_async_remote_copy(
            src_ref=src, dst_ref=dst, send_sem=ss, recv_sem=rs,
            device_id=did, device_id_type=MESH)

    def is_self(did):
        return (did[0] == r) & (did[1] == c) & (did[2] == d)

    own = list(dict.fromkeys([0, H]))
    far = [k for k in range(R) if k not in own]
    near = [k for k in range(R) if k not in own + far]
    spot = {k: n for n, k in enumerate(own + near + far)}
    cut1, cut2 = len(own) * PR, len(own + near) * PR

    def piece_at(x, k):
        return x.at[spot[k % R] * PR:(spot[k % R] + 1) * PR]

    def block_at(x, k, j):
        return x.at[pl.ds(pl.multiple_of(spot[k] * PR + j * BS, BS), BS)]

    def load(t):
        return pltpu.make_async_copy(
            p_hbm.at[:, :, pl.ds(t * LANES, LANES)], p.at[pl.ds(t * RB, RB)], load_sem.at[t])

    scatter = [
        (q, w, v, ((q + v * H) % R, r, side * half + w))
        for v in range(2) for q in range(C) for w in range(half)]
    receivers = [(z, r, side * half + w) for z in range(R) for w in range(half)]
    hops = [k for n in range(H // 2, 0, -1) for k in (n, R - n)]
    hops = list(dict.fromkeys(hops))
    turned = [(lax.rem(c + v * H, R), r, d) for v in range(2)]

    barrier = pltpu.get_barrier_semaphore()

    def hello(did):
        pl.semaphore_signal(barrier, inc=1, device_id=did, device_id_type=MESH)

    def hello_other(did):
        @pl.when(jnp.logical_not(is_self(did)))
        def _():
            hello(did)

    for e in range(D):
        hello_other((c, (d // half) * Y, lax.rem(d + e, D)))
    for v in range(2):
        hello_other((c, lax.rem(r + v * H, R), d))
    for k in hops:
        hello((lax.rem(r + k, R), c, d))
    hello(sibling)
    for k in range(Y):
        for e in range(D):
            if k or e:
                hello((r, 2 * lax.rem(y + k, Y) + core, lax.rem(d + e, D)))

    def others(dids):
        return sum(jnp.where(is_self(did), 0, 1) for did in dids)

    for t in range(T):
        load(t).start()

    row = lax.broadcasted_iota(jnp.int32, (RB, LANES), 0)
    place = lax.broadcasted_iota(jnp.int32, (RB, LANES), 1)
    local = cols[...] - c * RB
    code = jnp.full((RB, LANES), 2 * T * RB, jnp.int32)
    for u in range(RB):
        at = 2 * ((u // 2) * RB + row) + ((place & 1) ^ (u & 1))
        code = jnp.where(local[:, u:u + 1] == place, at, code)
    table[...] = code
    fill = pltpu.make_async_copy(table, codes, table_sem)
    fill.start()
    p[T * RB] = jnp.zeros((BS, LANES), jnp.bfloat16)
    panels = others(receivers)
    pl.semaphore_wait(
        barrier, len(hops) + Y * D + others(turned) + jnp.where(source, panels, 0))

    fill.wait()

    left = lax.broadcasted_iota(jnp.int32, (BS, LANES), 1) < BS

    def placed(i, j):
        def pick(code):
            tile = p[code >> 1]
            moved = jnp.concatenate([tile[:, BS:], tile[:, :BS]], axis=1)
            return jnp.where(jnp.full((BS, LANES), code & 1) == 1, moved, tile)

        return jnp.where(left, pick(codes[i, 2 * j]), pick(codes[i, 2 * j + 1]))

    for t in range(T):
        load(t).wait()

    def panel_copy(q, w, v, did):
        return remote(
            panel.at[q, w], block_at(x1, v * H, d), scat_send.at[q, w, v], in1.at[v], did)

    @pl.when(source)
    def _():
        def extract(q, _):
            for w in range(half):
                panel[q, w] = placed(q * PB + d, w)
            return 0

        lax.fori_loop(0, C, extract, 0)
        for s in scatter:
            @pl.when(is_self(s[-1]))
            def _(s=s):
                pltpu.make_async_copy(
                    panel.at[s[0], s[1]], block_at(x1, s[2] * H, d), in1.at[s[2]]).start()

            @pl.when(jnp.logical_not(is_self(s[-1])))
            def _(s=s):
                panel_copy(*s).start()

    starts = []
    for q in range(R):
        k = lax.rem(q - r + R, R)
        starts.append(sum(jnp.where(k == key, n * PR, 0) for key, n in spot.items()))

    def densify(i, _):
        rows = pl.ds(pl.multiple_of(i * BS, BS), BS)
        for j in range(T):
            q, within = j * R // T, j % (T // R) * LANES
            at = pl.ds(pl.multiple_of(starts[q] + within, LANES), LANES)
            dense[rows, at] = placed(i, j)
        return 0

    lax.fori_loop(0, RB, densify, 0)

    def partial(x, begin, end):
        def add(n, _):
            rows = pl.ds(pl.multiple_of(n * 2 * PR, 2 * PR), 2 * PR)
            term = jnp.dot(
                dense[rows, begin:end], x[begin:end, :], preferred_element_type=jnp.float32)
            part[rows, :] = term if begin == 0 else part[rows, :] + term
            return 0

        lax.fori_loop(0, C // 2, add, 0)

    def spread(x, arrived, sends, recvs):
        def copy(v, k):
            return remote(
                piece_at(x, v * H), piece_at(x, v * H - k), sends.at[v, k], recvs.at[v, k],
                (lax.rem(r + k, R), c, d))

        moves = [(v, k) for v in range(2) for k in hops if v == 0 or 2 * min(k, R - k) < H]
        for v in range(2):
            at = piece_at(x, v * H)
            pltpu.make_async_copy(at, at, arrived.at[v]).wait()
            for move in moves:
                if move[0] == v:
                    copy(*move).start()
        partial(x, 0, cut1)
        if cut2 > cut1:
            for move in moves:
                if (move[0] * H - move[1]) % R in near:
                    copy(*move).wait_recv()
            partial(x, cut1, cut2)
        for move in moves:
            if (move[0] * H - move[1]) % R in far:
                copy(*move).wait_recv()
        return [copy(*move) for move in moves]

    def rows_of(q):
        return pl.ds(pl.multiple_of(q * PR, PR), PR)

    def product(x, q):
        total = part[rows_of(q), :]
        if far:
            total = total + jnp.dot(
                dense[rows_of(q), cut2:], x[cut2:, :], preferred_element_type=jnp.float32)
        return total

    def code(value, ref):
        n = value.shape[1]
        top = jnp.maximum(jnp.max(jnp.abs(value), axis=1, keepdims=True), 1e-30)
        level = jnp.ceil(jnp.log2(top) * 16.0) + 1.0
        scaled = jnp.round(value * (jnp.exp2(level * -0.0625) * 32000.0))
        ref[:, 0:n, :] = scaled.astype(jnp.int32).astype(jnp.int16)
        ref[:, n:n + 16, :] = jnp.broadcast_to(
            level, (value.shape[0], 16, LANES)).astype(jnp.int32).astype(jnp.int16)

    def decode(ref, n):
        level = ref[:, n:n + 16, :].astype(jnp.int32).astype(jnp.float32)[:, 0:1, :]
        scale = jnp.exp2(level * 0.0625) * (1.0 / 32000.0)
        return ref[:, 0:n, :].astype(jnp.int32).astype(jnp.float32) * scale

    turns = sorted(range(1, Y), key=lambda k: -min(k, Y - k)) + [0]

    def to_sibling(x, k, buffer, sends, recvs):
        m = lax.rem(y + k, Y)
        q = 2 * m + 1 - core
        return q, remote(part.at[rows_of(q)], buffer.at[k], sends.at[k], recvs.at[k], sibling)

    def with_sibling(x, buffer, sends, recvs, then):
        for k in turns:
            q, copy = to_sibling(x, k, buffer, sends, recvs)
            part[rows_of(q), :] = product(x, q)
            copy.start()
        for k in turns:
            q = 2 * lax.rem(y + k, Y) + core
            value = product(x, q)
            to_sibling(x, k, buffer, sends, recvs)[1].wait_recv()
            then(k, q, value + buffer[k])

    sent1 = spread(x1, in1, ag1_send, ag1_recv)

    def reduce1(k):
        q = 2 * lax.rem(y + k, Y) + core
        return remote(sent.at[k], recv.at[k], rs_send.at[k], rs_recv.at[k], (r, q, d))

    def send1(k, q, value):
        if k:
            code(value[None], sent.at[pl.ds(k, 1)])
            reduce1(k).start()
        else:
            square[...] = value

    with_sibling(x1, core1, core1_send, core1_recv, send1)
    total = square[...]
    for k in range(1, Y):
        reduce1(k).wait_recv()
        total = total + decode(recv.at[pl.ds(k, 1)], PR)[0]
    square[...] = total
    rounded[...] = total.astype(jnp.bfloat16)

    def turn(v):
        return remote(rounded, piece_at(x2, v * H), turn_send.at[v], in2.at[v], turned[v])

    for v in range(2):
        @pl.when(is_self(turned[v]))
        def _(v=v):
            pltpu.make_async_copy(rounded, piece_at(x2, v * H), in2.at[v]).start()

        @pl.when(jnp.logical_not(is_self(turned[v])))
        def _(v=v):
            turn(v).start()

    def give(e):
        to = lax.rem(d + e, D)
        return remote(
            square.at[pl.ds(pl.multiple_of(to * BS, BS), BS)], owned.at[d],
            sq_send.at[e], sq_recv.at[e], (r, c, to))

    for k in range(Y):
        to_sibling(x1, k, core1, core1_send, core1_recv)[1].wait_send()
        if k:
            reduce1(k).wait_send()
    sent2 = spread(x2, in2, ag2_send, ag2_recv)
    for e in range(1, D):
        give(e).start()

    def cube(k, e):
        q, to = 2 * lax.rem(y + k, Y) + core, lax.rem(d + e, D)
        return remote(
            shares.at[k, to], cubes.at[y * D + d],
            cu_send.at[k * D + e], cu_recv, (r, q, to))

    def send2(k, q, value):
        code(value.reshape(D, BS, LANES), shares.at[k])
        for e in sorted(range(D), key=lambda e: -min(e, D - e)):
            if k or e:
                cube(k, e).start()
            else:
                pltpu.make_async_copy(shares.at[0, d], cubes.at[y * D + d], cu_recv).start()

    with_sibling(x2, core2, core2_send, core2_recv, send2)
    for e in range(1, D):
        give(e).wait_recv()
    pltpu.make_async_copy(cubes, cubes, cu_recv).wait()
    mine = square[pl.ds(pl.multiple_of(d * BS, BS), BS), :]
    sums = decode(cubes.at[pl.ds(0, D)], BS)
    for m in range(1, Y):
        sums = sums + decode(cubes.at[pl.ds(m * D, D)], BS)
    for e in range(D):
        total = sums[e]
        out[:, e * LANES:(e + 1) * LANES] = 3.0 * jnp.where(d == e, mine, owned[e]) - 2.0 * total

    @pl.when(source)
    def _():
        for s in scatter:
            @pl.when(jnp.logical_not(is_self(s[-1])))
            def _(s=s):
                panel_copy(*s).wait_send()

    for copy in sent1 + sent2:
        copy.wait_send()
    for v in range(2):
        @pl.when(jnp.logical_not(is_self(turned[v])))
        def _(v=v):
            turn(v).wait_send()

    for e in range(1, D):
        give(e).wait_send()
    for k in range(Y):
        to_sibling(x2, k, core2, core2_send, core2_recv)[1].wait_send()
        for e in range(D):
            if k or e:
                cube(k, e).wait_send()


def body(p_blocks, p_cols, out_mask):
    R, C, D = lax.axis_size("row"), lax.axis_size("col"), lax.axis_size("depth")
    RB, BS, K = p_blocks.shape
    WB = out_mask.shape[1]
    PR = RB // C * BS
    T, Y = K // LANES, C // 2
    bf, f32 = jnp.bfloat16, jnp.float32
    dma = pltpu.SemaphoreType.DMA
    rows = pl.pallas_call(
        functools.partial(kernel, R, C, D, RB, BS),
        out_shape=jax.ShapeDtypeStruct((BS, WB * BS), f32),
        in_specs=[pl.BlockSpec(memory_space=pl.ANY), pl.BlockSpec(memory_space=pltpu.VMEM)],
        out_specs=pl.BlockSpec(memory_space=pltpu.VMEM),
        scratch_shapes=[
            pltpu.VMEM((RB, LANES), jnp.int32),
            pltpu.SMEM((RB, LANES), jnp.int32),
            pltpu.VMEM((T * RB + 1, BS, LANES), bf),
            pltpu.VMEM((K, K), bf),
            pltpu.VMEM((C, D // 2, BS, LANES), bf),
            pltpu.VMEM((K, LANES), bf),
            pltpu.VMEM((K, LANES), bf),
            pltpu.VMEM((K, LANES), f32),
            pltpu.VMEM((Y, PR, LANES), f32),
            pltpu.VMEM((Y, PR, LANES), f32),
            pltpu.VMEM((Y, PR + 16, LANES), jnp.int16),
            pltpu.VMEM((Y, PR + 16, LANES), jnp.int16),
            pltpu.VMEM((PR, LANES), f32),
            pltpu.VMEM((PR, LANES), bf),
            pltpu.VMEM((Y, D, BS + 16, LANES), jnp.int16),
            pltpu.VMEM((Y * D, BS + 16, LANES), jnp.int16),
            pltpu.VMEM((D, BS, LANES), f32),
            dma, dma((T,)), dma((C, D // 2, 2)), dma((2,)), dma((2, R)), dma((2, R)),
            dma((Y,)), dma((Y,)), dma((Y,)), dma((Y,)),
            dma((2,)), dma((2,)), dma((2, R)), dma((2, R)), dma((D,)), dma((D,)),
            dma((Y,)), dma((Y,)), dma((Y * D,)), dma,
        ],
        compiler_params=pltpu.CompilerParams(
            collective_id=0, has_side_effects=True, vmem_limit_bytes=48 << 20),
    )(p_blocks, p_cols)
    kept = jnp.repeat(out_mask.astype(f32), BS, axis=1)
    return (rows * kept).reshape(1, BS, WB * BS)


def solution(mesh):
    in_specs = (P("row", None, "col"), P("row", "col"), P(("row", "col", "depth"), None))
    out_specs = P(("row", "col", "depth"), None, None)
    return jax.shard_map(body, mesh=mesh, in_specs=in_specs, out_specs=out_specs, check_vma=False)
```

```python
import functools

import jax
import jax.numpy as jnp
from jax import lax
from jax.experimental import pallas as pl
from jax.experimental.pallas import tpu as pltpu
from jax.sharding import PartitionSpec as P

MESH = pl.DeviceIdType.MESH
LANES = 128


def kernel(
    R, C, D, RB, BS,
    p_hbm, cols, out,
    table, codes, p, dense, panel, x1, x2, part, core1, core2, sent, recv, square, rounded, shares, cubes, owned,
    table_sem, load_sem, scat_send, in1, ag1_send, ag1_recv, core1_send, core1_recv, rs_send, rs_recv,
    turn_send, in2, ag2_send, ag2_recv, sq_send, sq_recv, core2_send, core2_recv,
    cu_send, cu_recv,
):
    r, c, d = lax.axis_index("row"), lax.axis_index("col"), lax.axis_index("depth")
    PB = RB // C
    PR = PB * BS
    K = RB * BS
    T = K // LANES
    H, Y, half = R // 2, C // 2, D // 2
    y, core = c // 2, lax.rem(c, 2)
    sibling = (r, c + 1 - 2 * core, d)
    side = c // Y
    source = lax.rem(c, Y) == 0

    def remote(src, dst, ss, rs, did):
        return pltpu.make_async_remote_copy(
            src_ref=src, dst_ref=dst, send_sem=ss, recv_sem=rs,
            device_id=did, device_id_type=MESH)

    def is_self(did):
        return (did[0] == r) & (did[1] == c) & (did[2] == d)

    own = list(dict.fromkeys([0, H]))
    far = [k for k in range(R) if k not in own]
    near = [k for k in range(R) if k not in own + far]
    spot = {k: n for n, k in enumerate(own + near + far)}
    cut1, cut2 = len(own) * PR, len(own + near) * PR

    def piece_at(x, k):
        return x.at[spot[k % R] * PR:(spot[k % R] + 1) * PR]

    def block_at(x, k, j):
        return x.at[pl.ds(pl.multiple_of(spot[k] * PR + j * BS, BS), BS)]

    def load(t):
        return pltpu.make_async_copy(
            p_hbm.at[:, :, pl.ds(t * LANES, LANES)], p.at[pl.ds(t * RB, RB)], load_sem.at[t])

    scatter = [
        (lax.rem(r + k + R - v * H, R), w, v, k, (lax.rem(r + k, R), r, side * half + w))
        for v in range(2) for k in range(R) for w in range(half)]
    receivers = [(z, r, side * half + w) for z in range(R) for w in range(half)]
    hops = [k for n in range(H // 2, 0, -1) for k in (n, R - n)]
    hops = list(dict.fromkeys(hops))
    turned = [(lax.rem(c + v * H, R), r, d) for v in range(2)]

    barrier = pltpu.get_barrier_semaphore()

    def hello(did):
        pl.semaphore_signal(barrier, inc=1, device_id=did, device_id_type=MESH)

    def hello_other(did):
        @pl.when(jnp.logical_not(is_self(did)))
        def _():
            hello(did)

    for e in range(D):
        hello_other((c, (d // half) * Y, lax.rem(d + e, D)))
    for v in range(2):
        hello_other((c, lax.rem(r + v * H, R), d))
    for k in hops:
        hello((lax.rem(r + k, R), c, d))
    hello(sibling)
    for k in range(Y):
        for e in range(D):
            if k or e:
                hello((r, 2 * lax.rem(y + k, Y) + core, lax.rem(d + e, D)))

    def others(dids):
        return sum(jnp.where(is_self(did), 0, 1) for did in dids)

    for t in range(T):
        load(t).start()

    row = lax.broadcasted_iota(jnp.int32, (RB, LANES), 0)
    place = lax.broadcasted_iota(jnp.int32, (RB, LANES), 1)
    local = cols[...] - c * RB
    code = jnp.full((RB, LANES), 2 * T * RB, jnp.int32)
    for u in range(RB):
        at = 2 * ((u // 2) * RB + row) + ((place & 1) ^ (u & 1))
        code = jnp.where(local[:, u:u + 1] == place, at, code)
    table[...] = code
    fill = pltpu.make_async_copy(table, codes, table_sem)
    fill.start()
    p[T * RB] = jnp.zeros((BS, LANES), jnp.bfloat16)
    panels = others(receivers)
    pl.semaphore_wait(
        barrier, len(hops) + Y * D + others(turned) + jnp.where(source, panels, 0))

    fill.wait()

    left = lax.broadcasted_iota(jnp.int32, (BS, LANES), 1) < BS

    def placed(i, j):
        def pick(code):
            tile = p[code >> 1]
            moved = jnp.concatenate([tile[:, BS:], tile[:, :BS]], axis=1)
            return jnp.where(jnp.full((BS, LANES), code & 1) == 1, moved, tile)

        return jnp.where(left, pick(codes[i, 2 * j]), pick(codes[i, 2 * j + 1]))

    for t in range(T):
        load(t).wait()

    def panel_copy(q, w, v, k, did):
        return remote(
            panel.at[q, w], block_at(x1, v * H, d), scat_send.at[k, w, v], in1.at[v], did)

    @pl.when(source)
    def _():
        def extract(q, _):
            for w in range(half):
                panel[q, w] = placed(q * PB + d, w)
            return 0

        lax.fori_loop(0, C, extract, 0)
        for s in scatter:
            if s[3]:
                panel_copy(*s).start()
                continue

            @pl.when(is_self(s[-1]))
            def _(s=s):
                pltpu.make_async_copy(
                    panel.at[s[0], s[1]], block_at(x1, s[2] * H, d), in1.at[s[2]]).start()

            @pl.when(jnp.logical_not(is_self(s[-1])))
            def _(s=s):
                panel_copy(*s).start()

    starts = []
    for q in range(R):
        k = lax.rem(q - r + R, R)
        starts.append(sum(jnp.where(k == key, n * PR, 0) for key, n in spot.items()))

    def densify(i, _):
        rows = pl.ds(pl.multiple_of(i * BS, BS), BS)
        for j in range(T):
            q, within = j * R // T, j % (T // R) * LANES
            at = pl.ds(pl.multiple_of(starts[q] + within, LANES), LANES)
            dense[rows, at] = placed(i, j)
        return 0

    lax.fori_loop(0, RB, densify, 0)

    def partial(x, begin, end):
        def add(n, _):
            rows = pl.ds(pl.multiple_of(n * 2 * PR, 2 * PR), 2 * PR)
            term = jnp.dot(
                dense[rows, begin:end], x[begin:end, :], preferred_element_type=jnp.float32)
            part[rows, :] = term if begin == 0 else part[rows, :] + term
            return 0

        lax.fori_loop(0, C // 2, add, 0)

    def spread(x, arrived, sends, recvs):
        def copy(v, k):
            return remote(
                piece_at(x, v * H), piece_at(x, v * H - k), sends.at[v, k], recvs.at[v, k],
                (lax.rem(r + k, R), c, d))

        moves = [(v, k) for v in range(2) for k in hops if v == 0 or 2 * min(k, R - k) < H]
        for v in range(2):
            at = piece_at(x, v * H)
            pltpu.make_async_copy(at, at, arrived.at[v]).wait()
            for move in moves:
                if move[0] == v:
                    copy(*move).start()
        partial(x, 0, cut1)
        if cut2 > cut1:
            for move in moves:
                if (move[0] * H - move[1]) % R in near:
                    copy(*move).wait_recv()
            partial(x, cut1, cut2)
        for move in moves:
            if (move[0] * H - move[1]) % R in far:
                copy(*move).wait_recv()
        return [copy(*move) for move in moves]

    def rows_of(q):
        return pl.ds(pl.multiple_of(q * PR, PR), PR)

    def product(x, q):
        total = part[rows_of(q), :]
        if far:
            total = total + jnp.dot(
                dense[rows_of(q), cut2:], x[cut2:, :], preferred_element_type=jnp.float32)
        return total

    def code(value, ref):
        n = value.shape[1]
        top = jnp.maximum(jnp.max(jnp.abs(value), axis=1, keepdims=True), 1e-30)
        level = jnp.ceil(jnp.log2(top) * 16.0) + 1.0
        scaled = jnp.round(value * (jnp.exp2(level * -0.0625) * 32000.0))
        ref[:, 0:n, :] = scaled.astype(jnp.int32).astype(jnp.int16)
        ref[:, n:n + 16, :] = jnp.broadcast_to(
            level, (value.shape[0], 16, LANES)).astype(jnp.int32).astype(jnp.int16)

    def decode(ref, n):
        level = ref[:, n:n + 16, :].astype(jnp.int32).astype(jnp.float32)[:, 0:1, :]
        scale = jnp.exp2(level * 0.0625) * (1.0 / 32000.0)
        return ref[:, 0:n, :].astype(jnp.int32).astype(jnp.float32) * scale

    turns = sorted(range(1, Y), key=lambda k: -min(k, Y - k)) + [0]

    def to_sibling(x, k, buffer, sends, recvs):
        m = lax.rem(y + k, Y)
        q = 2 * m + 1 - core
        return q, remote(part.at[rows_of(q)], buffer.at[k], sends.at[k], recvs.at[k], sibling)

    def with_sibling(x, buffer, sends, recvs, then):
        for k in turns:
            q, copy = to_sibling(x, k, buffer, sends, recvs)
            part[rows_of(q), :] = product(x, q)
            copy.start()
        for k in turns:
            q = 2 * lax.rem(y + k, Y) + core
            value = product(x, q)
            to_sibling(x, k, buffer, sends, recvs)[1].wait_recv()
            then(k, q, value + buffer[k])

    sent1 = spread(x1, in1, ag1_send, ag1_recv)

    def reduce1(k):
        q = 2 * lax.rem(y + k, Y) + core
        return remote(sent.at[k], recv.at[k], rs_send.at[k], rs_recv.at[k], (r, q, d))

    def send1(k, q, value):
        if k:
            code(value[None], sent.at[pl.ds(k, 1)])
            reduce1(k).start()
        else:
            square[...] = value

    with_sibling(x1, core1, core1_send, core1_recv, send1)
    total = square[...]
    for k in range(1, Y):
        reduce1(k).wait_recv()
        total = total + decode(recv.at[pl.ds(k, 1)], PR)[0]
    square[...] = total
    rounded[...] = total.astype(jnp.bfloat16)

    def turn(v):
        return remote(rounded, piece_at(x2, v * H), turn_send.at[v], in2.at[v], turned[v])

    for v in range(2):
        @pl.when(is_self(turned[v]))
        def _(v=v):
            pltpu.make_async_copy(rounded, piece_at(x2, v * H), in2.at[v]).start()

        @pl.when(jnp.logical_not(is_self(turned[v])))
        def _(v=v):
            turn(v).start()

    def give(e):
        to = lax.rem(d + e, D)
        return remote(
            square.at[pl.ds(pl.multiple_of(to * BS, BS), BS)], owned.at[d],
            sq_send.at[e], sq_recv.at[e], (r, c, to))

    for k in range(Y):
        to_sibling(x1, k, core1, core1_send, core1_recv)[1].wait_send()
        if k:
            reduce1(k).wait_send()
    sent2 = spread(x2, in2, ag2_send, ag2_recv)
    for e in range(1, D):
        give(e).start()

    def cube(k, e):
        q, to = 2 * lax.rem(y + k, Y) + core, lax.rem(d + e, D)
        return remote(
            shares.at[k, to], cubes.at[y * D + d],
            cu_send.at[k * D + e], cu_recv, (r, q, to))

    def send2(k, q, value):
        code(value.reshape(D, BS, LANES), shares.at[k])
        for e in sorted(range(D), key=lambda e: -min(e, D - e)):
            if k or e:
                cube(k, e).start()
            else:
                pltpu.make_async_copy(shares.at[0, d], cubes.at[y * D + d], cu_recv).start()

    with_sibling(x2, core2, core2_send, core2_recv, send2)
    for e in range(1, D):
        give(e).wait_recv()
    pltpu.make_async_copy(cubes, cubes, cu_recv).wait()
    mine = square[pl.ds(pl.multiple_of(d * BS, BS), BS), :]
    sums = decode(cubes.at[pl.ds(0, D)], BS)
    for m in range(1, Y):
        sums = sums + decode(cubes.at[pl.ds(m * D, D)], BS)
    for e in range(D):
        total = sums[e]
        out[:, e * LANES:(e + 1) * LANES] = 3.0 * jnp.where(d == e, mine, owned[e]) - 2.0 * total

    @pl.when(source)
    def _():
        for s in scatter:
            if s[3]:
                panel_copy(*s).wait_send()
                continue

            @pl.when(jnp.logical_not(is_self(s[-1])))
            def _(s=s):
                panel_copy(*s).wait_send()

    for copy in sent1 + sent2:
        copy.wait_send()
    for v in range(2):
        @pl.when(jnp.logical_not(is_self(turned[v])))
        def _(v=v):
            turn(v).wait_send()

    for e in range(1, D):
        give(e).wait_send()
    for k in range(Y):
        to_sibling(x2, k, core2, core2_send, core2_recv)[1].wait_send()
        for e in range(D):
            if k or e:
                cube(k, e).wait_send()


def body(p_blocks, p_cols, out_mask):
    R, C, D = lax.axis_size("row"), lax.axis_size("col"), lax.axis_size("depth")
    RB, BS, K = p_blocks.shape
    WB = out_mask.shape[1]
    PR = RB // C * BS
    T, Y = K // LANES, C // 2
    bf, f32 = jnp.bfloat16, jnp.float32
    dma = pltpu.SemaphoreType.DMA
    rows = pl.pallas_call(
        functools.partial(kernel, R, C, D, RB, BS),
        out_shape=jax.ShapeDtypeStruct((BS, WB * BS), f32),
        in_specs=[pl.BlockSpec(memory_space=pl.ANY), pl.BlockSpec(memory_space=pltpu.VMEM)],
        out_specs=pl.BlockSpec(memory_space=pltpu.VMEM),
        scratch_shapes=[
            pltpu.VMEM((RB, LANES), jnp.int32),
            pltpu.SMEM((RB, LANES), jnp.int32),
            pltpu.VMEM((T * RB + 1, BS, LANES), bf),
            pltpu.VMEM((K, K), bf),
            pltpu.VMEM((C, D // 2, BS, LANES), bf),
            pltpu.VMEM((K, LANES), bf),
            pltpu.VMEM((K, LANES), bf),
            pltpu.VMEM((K, LANES), f32),
            pltpu.VMEM((Y, PR, LANES), f32),
            pltpu.VMEM((Y, PR, LANES), f32),
            pltpu.VMEM((Y, PR + 16, LANES), jnp.int16),
            pltpu.VMEM((Y, PR + 16, LANES), jnp.int16),
            pltpu.VMEM((PR, LANES), f32),
            pltpu.VMEM((PR, LANES), bf),
            pltpu.VMEM((Y, D, BS + 16, LANES), jnp.int16),
            pltpu.VMEM((Y * D, BS + 16, LANES), jnp.int16),
            pltpu.VMEM((D, BS, LANES), f32),
            dma, dma((T,)), dma((C, D // 2, 2)), dma((2,)), dma((2, R)), dma((2, R)),
            dma((Y,)), dma((Y,)), dma((Y,)), dma((Y,)),
            dma((2,)), dma((2,)), dma((2, R)), dma((2, R)), dma((D,)), dma((D,)),
            dma((Y,)), dma((Y,)), dma((Y * D,)), dma,
        ],
        compiler_params=pltpu.CompilerParams(
            collective_id=0, has_side_effects=True, vmem_limit_bytes=48 << 20),
    )(p_blocks, p_cols)
    kept = jnp.repeat(out_mask.astype(f32), BS, axis=1)
    return (rows * kept).reshape(1, BS, WB * BS)


def solution(mesh):
    in_specs = (P("row", None, "col"), P("row", "col"), P(("row", "col", "depth"), None))
    out_specs = P(("row", "col", "depth"), None, None)
    return jax.shard_map(body, mesh=mesh, in_specs=in_specs, out_specs=out_specs, check_vma=False)
```

```python
import functools

import jax
import jax.numpy as jnp
from jax import lax
from jax.experimental import pallas as pl
from jax.experimental.pallas import tpu as pltpu
from jax.sharding import PartitionSpec as P

MESH = pl.DeviceIdType.MESH
LANES = 128


def kernel(
    R, C, D, RB, BS,
    p_hbm, cols, out,
    table, codes, p, dense, panel, x1, x2, part, core1, core2, sent, recv, square, rounded, shares, cubes, owned,
    table_sem, load_sem, scat_send, in1, ag1_send, ag1_recv, core1_send, core1_recv, rs_send, rs_recv,
    turn_send, in2, ag2_send, ag2_recv, sq_send, sq_recv, core2_send, core2_recv,
    cu_send, cu_recv,
):
    r, c, d = lax.axis_index("row"), lax.axis_index("col"), lax.axis_index("depth")
    PB = RB // C
    PR = PB * BS
    K = RB * BS
    T = K // LANES
    H, Y, half = R // 2, C // 2, D // 2
    y, core = c // 2, lax.rem(c, 2)
    sibling = (r, c + 1 - 2 * core, d)
    side = c // Y
    source = lax.rem(c, Y) == 0

    def remote(src, dst, ss, rs, did):
        return pltpu.make_async_remote_copy(
            src_ref=src, dst_ref=dst, send_sem=ss, recv_sem=rs,
            device_id=did, device_id_type=MESH)

    def is_self(did):
        return (did[0] == r) & (did[1] == c) & (did[2] == d)

    own = list(dict.fromkeys([0, H]))
    far = sorted((k for k in range(R) if k not in own), key=lambda k: k % 2)
    spot = {k: n for n, k in enumerate(own + far)}
    evens = list(range(0, R, 2))

    def piece_at(x, k):
        return x.at[spot[k % R] * PR:(spot[k % R] + 1) * PR]

    def block_at(x, k, j):
        return x.at[pl.ds(pl.multiple_of(spot[k] * PR + j * BS, BS), BS)]

    def load(t):
        return pltpu.make_async_copy(
            p_hbm.at[:, :, pl.ds(t * LANES, LANES)], p.at[pl.ds(t * RB, RB)], load_sem.at[t])

    scatter = [
        (q, w, v, ((q + v * H) % R, r, side * half + w))
        for v in range(2) for q in range(C) for w in range(half)]
    receivers = [(z, r, side * half + w) for z in range(R) for w in range(half)]
    hops = [k for n in range(H // 2, 0, -1) for k in (n, R - n)]
    hops = list(dict.fromkeys(hops))
    turned = [(lax.rem(c + o, R), r, d) for o in evens]

    barrier = pltpu.get_barrier_semaphore()

    def hello(did):
        pl.semaphore_signal(barrier, inc=1, device_id=did, device_id_type=MESH)

    def hello_other(did):
        @pl.when(jnp.logical_not(is_self(did)))
        def _():
            hello(did)

    for e in range(D):
        hello_other((c, (d // half) * Y, lax.rem(d + e, D)))
    for o in evens:
        hello_other((c, lax.rem(r + R - o, R), d))
    for k in hops:
        hello((lax.rem(r + k, R), c, d))
    hello(sibling)
    for k in range(Y):
        for e in range(D):
            if k or e:
                hello((r, 2 * lax.rem(y + k, Y) + core, lax.rem(d + e, D)))

    def others(dids):
        return sum(jnp.where(is_self(did), 0, 1) for did in dids)

    for t in range(T):
        load(t).start()

    row = lax.broadcasted_iota(jnp.int32, (RB, LANES), 0)
    place = lax.broadcasted_iota(jnp.int32, (RB, LANES), 1)
    local = cols[...] - c * RB
    code = jnp.full((RB, LANES), 2 * T * RB, jnp.int32)
    for u in range(RB):
        at = 2 * ((u // 2) * RB + row) + ((place & 1) ^ (u & 1))
        code = jnp.where(local[:, u:u + 1] == place, at, code)
    table[...] = code
    fill = pltpu.make_async_copy(table, codes, table_sem)
    fill.start()
    p[T * RB] = jnp.zeros((BS, LANES), jnp.bfloat16)
    panels = others(receivers)
    pl.semaphore_wait(
        barrier, len(hops) + Y * D + others(turned) + jnp.where(source, panels, 0))

    fill.wait()

    left = lax.broadcasted_iota(jnp.int32, (BS, LANES), 1) < BS

    def placed(i, j):
        def pick(code):
            tile = p[code >> 1]
            moved = jnp.concatenate([tile[:, BS:], tile[:, :BS]], axis=1)
            return jnp.where(jnp.full((BS, LANES), code & 1) == 1, moved, tile)

        return jnp.where(left, pick(codes[i, 2 * j]), pick(codes[i, 2 * j + 1]))

    for t in range(T):
        load(t).wait()

    def panel_copy(q, w, v, did):
        return remote(
            panel.at[q, w], block_at(x1, v * H, d), scat_send.at[q, w, v], in1.at[v], did)

    @pl.when(source)
    def _():
        def extract(q, _):
            for w in range(half):
                panel[q, w] = placed(q * PB + d, w)
            return 0

        lax.fori_loop(0, C, extract, 0)
        for s in scatter:
            @pl.when(is_self(s[-1]))
            def _(s=s):
                pltpu.make_async_copy(
                    panel.at[s[0], s[1]], block_at(x1, s[2] * H, d), in1.at[s[2]]).start()

            @pl.when(jnp.logical_not(is_self(s[-1])))
            def _(s=s):
                panel_copy(*s).start()

    starts = []
    for q in range(R):
        k = lax.rem(q - r + R, R)
        starts.append(sum(jnp.where(k == key, n * PR, 0) for key, n in spot.items()))

    def densify(i, _):
        rows = pl.ds(pl.multiple_of(i * BS, BS), BS)
        for j in range(T):
            q, within = j * R // T, j % (T // R) * LANES
            at = pl.ds(pl.multiple_of(starts[q] + within, LANES), LANES)
            dense[rows, at] = placed(i, j)
        return 0

    lax.fori_loop(0, RB, densify, 0)

    def partial(x, begin, end):
        def add(n, _):
            rows = pl.ds(pl.multiple_of(n * 2 * PR, 2 * PR), 2 * PR)
            term = jnp.dot(
                dense[rows, begin:end], x[begin:end, :], preferred_element_type=jnp.float32)
            part[rows, :] = term if begin == 0 else part[rows, :] + term
            return 0

        lax.fori_loop(0, C // 2, add, 0)

    def spread(x, held, moves, arrived, sends, recvs):
        def copy(n):
            o, k = moves[n]
            return remote(
                piece_at(x, o), piece_at(x, o - k), sends.at[n], recvs.at[n],
                (lax.rem(r + k, R), c, d))

        for v, o in enumerate(held):
            at = piece_at(x, o)
            pltpu.make_async_copy(at, at, arrived.at[v]).wait()
            for n, move in enumerate(moves):
                if move[0] == o:
                    copy(n).start()
        partial(x, 0, len(held) * PR)
        for n in range(len(moves)):
            copy(n).wait_recv()
        return [copy(n) for n in range(len(moves))]

    def rows_of(q):
        return pl.ds(pl.multiple_of(q * PR, PR), PR)

    def product(x, begin, q):
        return part[rows_of(q), :] + jnp.dot(
            dense[rows_of(q), begin:], x[begin:, :], preferred_element_type=jnp.float32)

    def code(value, ref):
        n = value.shape[1]
        top = jnp.maximum(jnp.max(jnp.abs(value), axis=1, keepdims=True), 1e-30)
        level = jnp.ceil(jnp.log2(top) * 16.0) + 1.0
        scaled = jnp.round(value * (jnp.exp2(level * -0.0625) * 32000.0))
        ref[:, 0:n, :] = scaled.astype(jnp.int32).astype(jnp.int16)
        ref[:, n:n + 16, :] = jnp.broadcast_to(
            level, (value.shape[0], 16, LANES)).astype(jnp.int32).astype(jnp.int16)

    def decode(ref, n):
        level = ref[:, n:n + 16, :].astype(jnp.int32).astype(jnp.float32)[:, 0:1, :]
        scale = jnp.exp2(level * 0.0625) * (1.0 / 32000.0)
        return ref[:, 0:n, :].astype(jnp.int32).astype(jnp.float32) * scale

    turns = sorted(range(1, Y), key=lambda k: -min(k, Y - k)) + [0]

    def to_sibling(x, k, buffer, sends, recvs):
        m = lax.rem(y + k, Y)
        q = 2 * m + 1 - core
        return q, remote(part.at[rows_of(q)], buffer.at[k], sends.at[k], recvs.at[k], sibling)

    def with_sibling(x, begin, buffer, sends, recvs, then):
        for k in turns:
            q, copy = to_sibling(x, k, buffer, sends, recvs)
            part[rows_of(q), :] = product(x, begin, q)
            copy.start()
        for k in turns:
            q = 2 * lax.rem(y + k, Y) + core
            value = product(x, begin, q)
            to_sibling(x, k, buffer, sends, recvs)[1].wait_recv()
            then(k, q, value + buffer[k])

    moves1 = [(0, k) for k in hops] + [(H, k) for k in hops if 2 * min(k, R - k) < H]
    moves2 = [(0, 1), (0, R - 1), (2, R - 1), (R - 2, 1)]
    sent1 = spread(x1, own, moves1, in1, ag1_send, ag1_recv)

    def reduce1(k):
        q = 2 * lax.rem(y + k, Y) + core
        return remote(sent.at[k], recv.at[k], rs_send.at[k], rs_recv.at[k], (r, q, d))

    def send1(k, q, value):
        if k:
            code(value[None], sent.at[pl.ds(k, 1)])
            reduce1(k).start()
        else:
            square[...] = value

    with_sibling(x1, 2 * PR, core1, core1_send, core1_recv, send1)
    total = square[...]
    for k in range(1, Y):
        reduce1(k).wait_recv()
        total = total + decode(recv.at[pl.ds(k, 1)], PR)[0]
    square[...] = total
    rounded[...] = total.astype(jnp.bfloat16)

    def turn(v):
        return remote(rounded, piece_at(x2, -2 * v), turn_send.at[v], in2.at[-v % len(evens)], turned[v])

    for v in range(len(evens)):
        @pl.when(is_self(turned[v]))
        def _(v=v):
            pltpu.make_async_copy(rounded, piece_at(x2, -2 * v), in2.at[-v % len(evens)]).start()

        @pl.when(jnp.logical_not(is_self(turned[v])))
        def _(v=v):
            turn(v).start()

    def give(e):
        to = lax.rem(d + e, D)
        return remote(
            square.at[pl.ds(pl.multiple_of(to * BS, BS), BS)], owned.at[d],
            sq_send.at[e], sq_recv.at[e], (r, c, to))

    for k in range(Y):
        to_sibling(x1, k, core1, core1_send, core1_recv)[1].wait_send()
        if k:
            reduce1(k).wait_send()
    sent2 = spread(x2, evens, moves2, in2, ag2_send, ag2_recv)
    for e in range(1, D):
        give(e).start()

    def cube(k, e):
        q, to = 2 * lax.rem(y + k, Y) + core, lax.rem(d + e, D)
        return remote(
            shares.at[k, to], cubes.at[y * D + d],
            cu_send.at[k * D + e], cu_recv, (r, q, to))

    def send2(k, q, value):
        code(value.reshape(D, BS, LANES), shares.at[k])
        for e in sorted(range(D), key=lambda e: -min(e, D - e)):
            if k or e:
                cube(k, e).start()
            else:
                pltpu.make_async_copy(shares.at[0, d], cubes.at[y * D + d], cu_recv).start()

    with_sibling(x2, len(evens) * PR, core2, core2_send, core2_recv, send2)
    for e in range(1, D):
        give(e).wait_recv()
    pltpu.make_async_copy(cubes, cubes, cu_recv).wait()
    mine = square[pl.ds(pl.multiple_of(d * BS, BS), BS), :]
    sums = decode(cubes.at[pl.ds(0, D)], BS)
    for m in range(1, Y):
        sums = sums + decode(cubes.at[pl.ds(m * D, D)], BS)
    for e in range(D):
        total = sums[e]
        out[:, e * LANES:(e + 1) * LANES] = 3.0 * jnp.where(d == e, mine, owned[e]) - 2.0 * total

    @pl.when(source)
    def _():
        for s in scatter:
            @pl.when(jnp.logical_not(is_self(s[-1])))
            def _(s=s):
                panel_copy(*s).wait_send()

    for copy in sent1 + sent2:
        copy.wait_send()
    for v in range(len(evens)):
        @pl.when(jnp.logical_not(is_self(turned[v])))
        def _(v=v):
            turn(v).wait_send()

    for e in range(1, D):
        give(e).wait_send()
    for k in range(Y):
        to_sibling(x2, k, core2, core2_send, core2_recv)[1].wait_send()
        for e in range(D):
            if k or e:
                cube(k, e).wait_send()


def body(p_blocks, p_cols, out_mask):
    R, C, D = lax.axis_size("row"), lax.axis_size("col"), lax.axis_size("depth")
    RB, BS, K = p_blocks.shape
    WB = out_mask.shape[1]
    PR = RB // C * BS
    T, Y = K // LANES, C // 2
    bf, f32 = jnp.bfloat16, jnp.float32
    dma = pltpu.SemaphoreType.DMA
    rows = pl.pallas_call(
        functools.partial(kernel, R, C, D, RB, BS),
        out_shape=jax.ShapeDtypeStruct((BS, WB * BS), f32),
        in_specs=[pl.BlockSpec(memory_space=pl.ANY), pl.BlockSpec(memory_space=pltpu.VMEM)],
        out_specs=pl.BlockSpec(memory_space=pltpu.VMEM),
        scratch_shapes=[
            pltpu.VMEM((RB, LANES), jnp.int32),
            pltpu.SMEM((RB, LANES), jnp.int32),
            pltpu.VMEM((T * RB + 1, BS, LANES), bf),
            pltpu.VMEM((K, K), bf),
            pltpu.VMEM((C, D // 2, BS, LANES), bf),
            pltpu.VMEM((K, LANES), bf),
            pltpu.VMEM((K, LANES), bf),
            pltpu.VMEM((K, LANES), f32),
            pltpu.VMEM((Y, PR, LANES), f32),
            pltpu.VMEM((Y, PR, LANES), f32),
            pltpu.VMEM((Y, PR + 16, LANES), jnp.int16),
            pltpu.VMEM((Y, PR + 16, LANES), jnp.int16),
            pltpu.VMEM((PR, LANES), f32),
            pltpu.VMEM((PR, LANES), bf),
            pltpu.VMEM((Y, D, BS + 16, LANES), jnp.int16),
            pltpu.VMEM((Y * D, BS + 16, LANES), jnp.int16),
            pltpu.VMEM((D, BS, LANES), f32),
            dma, dma((T,)), dma((C, D // 2, 2)), dma((2,)), dma((R,)), dma((R,)),
            dma((Y,)), dma((Y,)), dma((Y,)), dma((Y,)),
            dma((R // 2,)), dma((R // 2,)), dma((R,)), dma((R,)), dma((D,)), dma((D,)),
            dma((Y,)), dma((Y,)), dma((Y * D,)), dma,
        ],
        compiler_params=pltpu.CompilerParams(
            collective_id=0, has_side_effects=True, vmem_limit_bytes=48 << 20),
    )(p_blocks, p_cols)
    kept = jnp.repeat(out_mask.astype(f32), BS, axis=1)
    return (rows * kept).reshape(1, BS, WB * BS)


def solution(mesh):
    in_specs = (P("row", None, "col"), P("row", "col"), P(("row", "col", "depth"), None))
    out_specs = P(("row", "col", "depth"), None, None)
    return jax.shard_map(body, mesh=mesh, in_specs=in_specs, out_specs=out_specs, check_vma=False)
```

```python
import functools

import jax
import jax.numpy as jnp
from jax import lax
from jax.experimental import pallas as pl
from jax.experimental.pallas import tpu as pltpu
from jax.sharding import PartitionSpec as P

MESH = pl.DeviceIdType.MESH
LANES = 128


def kernel(
    R, C, D, RB, BS,
    p_hbm, cols, out,
    table, codes, p, dense, panel, x1, x2, part, core1, core2, sent, recv, square, rounded, shares, cubes, owned,
    table_sem, load_sem, scat_send, in1, ag1_send, ag1_recv, core1_send, core1_recv, rs_send, rs_recv,
    turn_send, in2, ag2_send, ag2_recv, sq_send, sq_recv, core2_send, core2_recv,
    cu_send, cu_recv,
):
    r, c, d = lax.axis_index("row"), lax.axis_index("col"), lax.axis_index("depth")
    PB = RB // C
    PR = PB * BS
    K = RB * BS
    T = K // LANES
    H, Y, half = R // 2, C // 2, D // 2
    y, core = c // 2, lax.rem(c, 2)
    sibling = (r, c + 1 - 2 * core, d)
    side = c // Y
    source = lax.rem(c, Y) == 0

    def remote(src, dst, ss, rs, did):
        return pltpu.make_async_remote_copy(
            src_ref=src, dst_ref=dst, send_sem=ss, recv_sem=rs,
            device_id=did, device_id_type=MESH)

    def is_self(did):
        return (did[0] == r) & (did[1] == c) & (did[2] == d)

    own = list(dict.fromkeys([0, H]))
    far = sorted((k for k in range(R) if k not in own), key=lambda k: k % 2)
    spot = {k: n for n, k in enumerate(own + far)}
    evens = list(range(0, R, 2))

    def piece_at(x, k):
        return x.at[spot[k % R] * PR:(spot[k % R] + 1) * PR]

    def block_at(x, k, j):
        return x.at[pl.ds(pl.multiple_of(spot[k] * PR + j * BS, BS), BS)]

    def load(t):
        return pltpu.make_async_copy(
            p_hbm.at[:, :, pl.ds(t * LANES, LANES)], p.at[pl.ds(t * RB, RB)], load_sem.at[t])

    scatter = [
        (q, w, v, ((q + v * H) % R, r, side * half + w))
        for v in range(2) for q in range(C) for w in range(half)]
    receivers = [(z, r, side * half + w) for z in range(R) for w in range(half)]
    hops = [k for n in range(H // 2, 0, -1) for k in (n, R - n)]
    hops = list(dict.fromkeys(hops))
    turned = [(lax.rem(c + o, R), r, d) for o in evens]

    barrier = pltpu.get_barrier_semaphore()

    def hello(did):
        pl.semaphore_signal(barrier, inc=1, device_id=did, device_id_type=MESH)

    def hello_other(did):
        @pl.when(jnp.logical_not(is_self(did)))
        def _():
            hello(did)

    for e in range(D):
        hello_other((c, (d // half) * Y, lax.rem(d + e, D)))
    for o in evens:
        hello_other((c, lax.rem(r + R - o, R), d))
    for k in hops:
        hello((lax.rem(r + k, R), c, d))
    hello(sibling)
    for k in range(Y):
        for e in range(D):
            if k or e:
                hello((r, 2 * lax.rem(y + k, Y) + core, lax.rem(d + e, D)))

    def others(dids):
        return sum(jnp.where(is_self(did), 0, 1) for did in dids)

    for t in range(T):
        load(t).start()

    row = lax.broadcasted_iota(jnp.int32, (RB, LANES), 0)
    place = lax.broadcasted_iota(jnp.int32, (RB, LANES), 1)
    local = cols[...] - c * RB
    code = jnp.full((RB, LANES), 2 * T * RB, jnp.int32)
    for u in range(RB):
        at = 2 * ((u // 2) * RB + row) + ((place & 1) ^ (u & 1))
        code = jnp.where(local[:, u:u + 1] == place, at, code)
    table[...] = code
    fill = pltpu.make_async_copy(table, codes, table_sem)
    fill.start()
    p[T * RB] = jnp.zeros((BS, LANES), jnp.bfloat16)
    panels = others(receivers)
    pl.semaphore_wait(
        barrier, len(hops) + Y * D + others(turned) + jnp.where(source, panels, 0))

    fill.wait()

    left = lax.broadcasted_iota(jnp.int32, (BS, LANES), 1) < BS

    def placed(i, j):
        def pick(code):
            tile = p[code >> 1]
            moved = jnp.concatenate([tile[:, BS:], tile[:, :BS]], axis=1)
            return jnp.where(jnp.full((BS, LANES), code & 1) == 1, moved, tile)

        return jnp.where(left, pick(codes[i, 2 * j]), pick(codes[i, 2 * j + 1]))

    for t in range(T):
        load(t).wait()

    def panel_copy(q, w, v, did):
        return remote(
            panel.at[q, w], block_at(x1, v * H, d), scat_send.at[q, w, v], in1.at[v], did)

    @pl.when(source)
    def _():
        def extract(q, _):
            for w in range(half):
                panel[q, w] = placed(q * PB + d, w)
            return 0

        lax.fori_loop(0, C, extract, 0)
        for s in scatter:
            @pl.when(is_self(s[-1]))
            def _(s=s):
                pltpu.make_async_copy(
                    panel.at[s[0], s[1]], block_at(x1, s[2] * H, d), in1.at[s[2]]).start()

            @pl.when(jnp.logical_not(is_self(s[-1])))
            def _(s=s):
                panel_copy(*s).start()

    starts = []
    for q in range(R):
        k = lax.rem(q - r + R, R)
        starts.append(sum(jnp.where(k == key, n * PR, 0) for key, n in spot.items()))

    def densify(i, _):
        rows = pl.ds(pl.multiple_of(i * BS, BS), BS)
        for j in range(T):
            q, within = j * R // T, j % (T // R) * LANES
            at = pl.ds(pl.multiple_of(starts[q] + within, LANES), LANES)
            dense[rows, at] = placed(i, j)
        return 0

    lax.fori_loop(0, RB, densify, 0)

    def partial(x, begin, end):
        def add(n, _):
            rows = pl.ds(pl.multiple_of(n * 2 * PR, 2 * PR), 2 * PR)
            term = jnp.dot(
                dense[rows, begin:end], x[begin:end, :], preferred_element_type=jnp.float32)
            part[rows, :] = term if begin == 0 else part[rows, :] + term
            return 0

        lax.fori_loop(0, C // 2, add, 0)

    def spread(x, held, moves, arrived, sends, recvs):
        def copy(n):
            o, k = moves[n]
            return remote(
                piece_at(x, o), piece_at(x, o - k), sends.at[n], recvs.at[n],
                (lax.rem(r + k, R), c, d))

        sent_on = [o for o, _ in moves]
        for v, o in sorted(enumerate(held), key=lambda held: held[1] not in sent_on):
            at = piece_at(x, o)
            pltpu.make_async_copy(at, at, arrived.at[v]).wait()
            for n, move in enumerate(moves):
                if move[0] == o:
                    copy(n).start()
        partial(x, 0, len(held) * PR)
        for n in range(len(moves)):
            copy(n).wait_recv()
        return [copy(n) for n in range(len(moves))]

    def rows_of(q):
        return pl.ds(pl.multiple_of(q * PR, PR), PR)

    def product(x, begin, q):
        return part[rows_of(q), :] + jnp.dot(
            dense[rows_of(q), begin:], x[begin:, :], preferred_element_type=jnp.float32)

    def code(value, ref):
        n = value.shape[1]
        top = jnp.maximum(jnp.max(jnp.abs(value), axis=1, keepdims=True), 1e-30)
        level = jnp.ceil(jnp.log2(top) * 16.0) + 1.0
        scaled = jnp.round(value * (jnp.exp2(level * -0.0625) * 32000.0))
        ref[:, 0:n, :] = scaled.astype(jnp.int32).astype(jnp.int16)
        ref[:, n:n + 16, :] = jnp.broadcast_to(
            level, (value.shape[0], 16, LANES)).astype(jnp.int32).astype(jnp.int16)

    def decode(ref, n):
        level = ref[:, n:n + 16, :].astype(jnp.int32).astype(jnp.float32)[:, 0:1, :]
        scale = jnp.exp2(level * 0.0625) * (1.0 / 32000.0)
        return ref[:, 0:n, :].astype(jnp.int32).astype(jnp.float32) * scale

    turns = sorted(range(1, Y), key=lambda k: -min(k, Y - k)) + [0]

    def to_sibling(x, k, buffer, sends, recvs):
        m = lax.rem(y + k, Y)
        q = 2 * m + 1 - core
        return q, remote(part.at[rows_of(q)], buffer.at[k], sends.at[k], recvs.at[k], sibling)

    def with_sibling(x, begin, buffer, sends, recvs, then):
        for k in turns:
            q, copy = to_sibling(x, k, buffer, sends, recvs)
            part[rows_of(q), :] = product(x, begin, q)
            copy.start()
        for k in turns:
            q = 2 * lax.rem(y + k, Y) + core
            value = product(x, begin, q)
            to_sibling(x, k, buffer, sends, recvs)[1].wait_recv()
            then(k, q, value + buffer[k])

    moves1 = [(0, k) for k in hops] + [(H, k) for k in hops if 2 * min(k, R - k) < H]
    moves2 = [(0, 1), (0, R - 1), (2, R - 1), (R - 2, 1)]
    sent1 = spread(x1, own, moves1, in1, ag1_send, ag1_recv)

    def reduce1(k):
        q = 2 * lax.rem(y + k, Y) + core
        return remote(sent.at[k], recv.at[k], rs_send.at[k], rs_recv.at[k], (r, q, d))

    def send1(k, q, value):
        if k:
            code(value[None], sent.at[pl.ds(k, 1)])
            reduce1(k).start()
        else:
            square[...] = value

    with_sibling(x1, 2 * PR, core1, core1_send, core1_recv, send1)
    total = square[...]
    for k in range(1, Y):
        reduce1(k).wait_recv()
        total = total + decode(recv.at[pl.ds(k, 1)], PR)[0]
    square[...] = total
    rounded[...] = total.astype(jnp.bfloat16)

    def turn(v):
        return remote(rounded, piece_at(x2, -2 * v), turn_send.at[v], in2.at[-v % len(evens)], turned[v])

    for v in sorted(range(len(evens)), key=lambda v: 2 * v == H):
        @pl.when(is_self(turned[v]))
        def _(v=v):
            pltpu.make_async_copy(rounded, piece_at(x2, -2 * v), in2.at[-v % len(evens)]).start()

        @pl.when(jnp.logical_not(is_self(turned[v])))
        def _(v=v):
            turn(v).start()

    def give(e):
        to = lax.rem(d + e, D)
        return remote(
            square.at[pl.ds(pl.multiple_of(to * BS, BS), BS)], owned.at[d],
            sq_send.at[e], sq_recv.at[e], (r, c, to))

    for k in range(Y):
        to_sibling(x1, k, core1, core1_send, core1_recv)[1].wait_send()
        if k:
            reduce1(k).wait_send()
    sent2 = spread(x2, evens, moves2, in2, ag2_send, ag2_recv)
    for e in range(1, D):
        give(e).start()

    def cube(k, e):
        q, to = 2 * lax.rem(y + k, Y) + core, lax.rem(d + e, D)
        return remote(
            shares.at[k, to], cubes.at[y * D + d],
            cu_send.at[k * D + e], cu_recv, (r, q, to))

    def send2(k, q, value):
        code(value.reshape(D, BS, LANES), shares.at[k])
        for e in sorted(range(D), key=lambda e: -min(e, D - e)):
            if k or e:
                cube(k, e).start()
            else:
                pltpu.make_async_copy(shares.at[0, d], cubes.at[y * D + d], cu_recv).start()

    with_sibling(x2, len(evens) * PR, core2, core2_send, core2_recv, send2)
    for e in range(1, D):
        give(e).wait_recv()
    pltpu.make_async_copy(cubes, cubes, cu_recv).wait()
    mine = square[pl.ds(pl.multiple_of(d * BS, BS), BS), :]
    sums = decode(cubes.at[pl.ds(0, D)], BS)
    for m in range(1, Y):
        sums = sums + decode(cubes.at[pl.ds(m * D, D)], BS)
    for e in range(D):
        total = sums[e]
        out[:, e * LANES:(e + 1) * LANES] = 3.0 * jnp.where(d == e, mine, owned[e]) - 2.0 * total

    @pl.when(source)
    def _():
        for s in scatter:
            @pl.when(jnp.logical_not(is_self(s[-1])))
            def _(s=s):
                panel_copy(*s).wait_send()

    for copy in sent1 + sent2:
        copy.wait_send()
    for v in range(len(evens)):
        @pl.when(jnp.logical_not(is_self(turned[v])))
        def _(v=v):
            turn(v).wait_send()

    for e in range(1, D):
        give(e).wait_send()
    for k in range(Y):
        to_sibling(x2, k, core2, core2_send, core2_recv)[1].wait_send()
        for e in range(D):
            if k or e:
                cube(k, e).wait_send()


def body(p_blocks, p_cols, out_mask):
    R, C, D = lax.axis_size("row"), lax.axis_size("col"), lax.axis_size("depth")
    RB, BS, K = p_blocks.shape
    WB = out_mask.shape[1]
    PR = RB // C * BS
    T, Y = K // LANES, C // 2
    bf, f32 = jnp.bfloat16, jnp.float32
    dma = pltpu.SemaphoreType.DMA
    rows = pl.pallas_call(
        functools.partial(kernel, R, C, D, RB, BS),
        out_shape=jax.ShapeDtypeStruct((BS, WB * BS), f32),
        in_specs=[pl.BlockSpec(memory_space=pl.ANY), pl.BlockSpec(memory_space=pltpu.VMEM)],
        out_specs=pl.BlockSpec(memory_space=pltpu.VMEM),
        scratch_shapes=[
            pltpu.VMEM((RB, LANES), jnp.int32),
            pltpu.SMEM((RB, LANES), jnp.int32),
            pltpu.VMEM((T * RB + 1, BS, LANES), bf),
            pltpu.VMEM((K, K), bf),
            pltpu.VMEM((C, D // 2, BS, LANES), bf),
            pltpu.VMEM((K, LANES), bf),
            pltpu.VMEM((K, LANES), bf),
            pltpu.VMEM((K, LANES), f32),
            pltpu.VMEM((Y, PR, LANES), f32),
            pltpu.VMEM((Y, PR, LANES), f32),
            pltpu.VMEM((Y, PR + 16, LANES), jnp.int16),
            pltpu.VMEM((Y, PR + 16, LANES), jnp.int16),
            pltpu.VMEM((PR, LANES), f32),
            pltpu.VMEM((PR, LANES), bf),
            pltpu.VMEM((Y, D, BS + 16, LANES), jnp.int16),
            pltpu.VMEM((Y * D, BS + 16, LANES), jnp.int16),
            pltpu.VMEM((D, BS, LANES), f32),
            dma, dma((T,)), dma((C, D // 2, 2)), dma((2,)), dma((R,)), dma((R,)),
            dma((Y,)), dma((Y,)), dma((Y,)), dma((Y,)),
            dma((R // 2,)), dma((R // 2,)), dma((R,)), dma((R,)), dma((D,)), dma((D,)),
            dma((Y,)), dma((Y,)), dma((Y * D,)), dma,
        ],
        compiler_params=pltpu.CompilerParams(
            collective_id=0, has_side_effects=True, vmem_limit_bytes=48 << 20),
    )(p_blocks, p_cols)
    kept = jnp.repeat(out_mask.astype(f32), BS, axis=1)
    return (rows * kept).reshape(1, BS, WB * BS)


def solution(mesh):
    in_specs = (P("row", None, "col"), P("row", "col"), P(("row", "col", "depth"), None))
    out_specs = P(("row", "col", "depth"), None, None)
    return jax.shard_map(body, mesh=mesh, in_specs=in_specs, out_specs=out_specs, check_vma=False)
```
